512 devices in a mesh: dp: 32 (over z_lo, y, core), tensor: 16 (over z_hi, x).
Axes of the slice: x: 4, y: 4, z: 16 (z_hi: 4, z_lo: 4; z = z_hi * 4 + z_lo), core: 2. Of those that a mesh axis runs over, the one named last changes fastest.
Arguments:
- control_in: bfloat16 [4096, 3072], P('dp'), may hold values from -6 to 6
- control_project: bfloat16 [3, 3072, 2048], P(None, 'dp', 'tensor'), may hold values from -1 to 1
- control_output: bfloat16 [3072, 2048], P('dp', 'tensor'), may hold values from -0.5 to 0.5
- query_gain: float32 [128], replicated, may hold values from 0.5 to 8
- key_gain: float32 [128], replicated, may hold values from 0.5 to 8
- base_hidden: bfloat16 [4096, 3072], P('dp'), may hold values from -4 to 4
- base_up: bfloat16 [3072, 6144], P('dp', 'tensor'), may hold values from -0.109375 to 0.109375
- base_down: bfloat16 [3072, 6144], P('dp', 'tensor'), may hold values from -0.078125 to 0.078125
- cotangent: bfloat16 [4096, 3072], P('dp'), may hold values from -6 to 6
Outputs:
- base_out: bfloat16 [4096, 3072], P(('dp', 'tensor'))
- feat_grad: bfloat16 [4096, 3072], P(('dp', 'tensor'))
The draws below stay inside these ranges and needn't reach their ends.
All inputs are finite; a program needn't handle non-finite values.
Results may differ from the reference program's by a relative error of at most 0.025.
The reference program's roundings to bfloat16 on the way count: a program that leaves them out, or rounds other values in their place, can miss the bound.
Values may be sent and summed in bfloat16 or wider, within the bound.
A program may use at most 64 MiB of HBM per device.

```python
import math
import jax
import jax.numpy as jnp
from jax import lax

D = 3072
HD = 128
HEADS = 16
FF = 6144
TOKENS = 4096
N_TENSOR = 16


def spread_log(key, low_end, high_end):
    exponent = jax.random.uniform(key, (HD,), jnp.float32, math.log(low_end), math.log(high_end))
    return jnp.exp(exponent)


def draw_control_in(key, part):
    key = jax.random.fold_in(key, 11)
    drawn = jax.random.normal(key, (TOKENS, D), jnp.float32)
    return jnp.clip(drawn, -6.0, 6.0).astype(jnp.bfloat16)


def draw_control_project(key, part):
    key = jax.random.fold_in(key, 12)
    columns = HEADS * HD
    drawn = jnp.clip(jax.random.normal(key, (3, D, columns), jnp.float32), -6.0, 6.0) * D ** (-0.5)
    return drawn.astype(jnp.bfloat16)


def draw_query_gain(key, part):
    key = jax.random.fold_in(key, 13)
    return spread_log(key, 0.5, 2.0)


def draw_key_gain(key, part):
    key = jax.random.fold_in(key, 14)
    return spread_log(key, 0.5, 2.0)


def shard_levels(rng, shape, shards, least, largest):
    level = 1.0
    for position, shards_of in shards:
        steps = jax.random.uniform(jax.random.fold_in(jax.random.fold_in(rng, 6), position), (shards_of,), jnp.float32, least / len(shards), largest / len(shards))
        level = level * jnp.repeat(jnp.exp(steps), shape[position] // shards_of).reshape((-1,) + (1,) * (len(shape) - 1 - position))
    return level


def noise(rng, extent, scale, limit, cuts=(), kind=jnp.bfloat16):
    level = shard_levels(rng, extent, cuts, -0.22, 0.18) if cuts else 1.0
    result = jax.random.normal(rng, extent, jnp.float32) * scale * level
    return jnp.minimum(jnp.maximum(result, -limit), limit).astype(kind)


def setup_inputs(seed: int = 0) -> dict:
    arg_keys = jax.random.split(jax.random.key(seed), 10)
    return {
        "control_in": draw_control_in(jax.random.fold_in(arg_keys[9], 71), 0),
        "control_project": draw_control_project(jax.random.fold_in(arg_keys[9], 71), 0),
        "control_output": noise(arg_keys[2], (D, HEADS * HD), HD ** -0.5, 0.5, ((0, 32), (1, 16))),
        "query_gain": draw_query_gain(jax.random.fold_in(arg_keys[9], 71), 0),
        "key_gain": draw_key_gain(jax.random.fold_in(arg_keys[9], 71), 0),
        "base_hidden": noise(arg_keys[5], (TOKENS, D), 0.5, 4.0, ((0, 32),)),
        "base_up": noise(arg_keys[6], (D, FF), D ** -0.5, 0.109375, ((0, 32), (1, 16))),
        "base_down": noise(arg_keys[7], (D, FF), FF ** -0.5, 0.078125, ((0, 32), (1, 16))),
        "cotangent": noise(arg_keys[8], (TOKENS, D), 1.0, 6.0, ((0, 32),)),
    }


def norm_rows(values):
    center = values - lax.optimization_barrier(jnp.mean(values, axis=-1, keepdims=True))
    spread = lax.optimization_barrier(jnp.mean(center * center, axis=-1, keepdims=True))
    rstd = lax.rsqrt(spread + 1e-06)
    return (center * rstd, rstd)

def gelu_tanh(values):
    inner = 0.7978845608028654 * (values + 0.044715 * values * values * values)
    return 0.5 * values * (1.0 + jnp.tanh(inner))

def gelu_slope(values):
    inner = 0.7978845608028654 * (values + 0.044715 * values * values * values)
    tangent = jnp.tanh(inner)
    return 0.5 * (1.0 + tangent) + 0.5 * values * (1.0 - tangent * tangent) * 0.7978845608028654 * (1.0 + 3.0 * 0.044715 * values * values)

def times_transposed(left, right):
    return lax.dot_general(left, right, (((1,), (1,)), ((), ())), preferred_element_type=jnp.float32)

def head_norm(values, gain):
    split = values.reshape(TOKENS, HEADS, HD)
    square_mean = lax.optimization_barrier(jnp.mean(split * split, axis=-1, keepdims=True))
    normed = (split * lax.rsqrt(square_mean + 1e-06) * gain).astype(jnp.bfloat16)
    return jnp.transpose(normed, (1, 0, 2))

def reference(control_in, control_project, control_output, query_gain, key_gain, base_hidden, base_up, base_down, cotangent):
    normed_in = norm_rows(control_in.astype(jnp.float32))[0].astype(jnp.bfloat16)
    queries = head_norm(jnp.dot(normed_in, control_project[0], preferred_element_type=jnp.float32), query_gain)
    keys = head_norm(jnp.dot(normed_in, control_project[1], preferred_element_type=jnp.float32), key_gain)
    values = jnp.dot(normed_in, control_project[2], preferred_element_type=jnp.float32).astype(jnp.bfloat16)
    values = jnp.transpose(values.reshape(TOKENS, HEADS, HD), (1, 0, 2))
    score_scale = 1.0 / HD ** 0.5

    def one_head(operands):
        query_head, key_head, value_head = operands
        scores = times_transposed(query_head, key_head) * score_scale
        top = lax.optimization_barrier(jnp.max(scores, axis=1, keepdims=True))
        expo = jnp.exp(scores - top)
        total = lax.optimization_barrier(jnp.sum(expo, axis=1, keepdims=True))
        accum = jnp.dot(expo.astype(jnp.bfloat16), value_head, preferred_element_type=jnp.float32)
        return (accum / total).astype(jnp.bfloat16)
    mixed = lax.map(one_head, (queries, keys, values))
    mixed = jnp.transpose(mixed, (1, 0, 2)).reshape(TOKENS, HEADS * HD)
    features = times_transposed(mixed, control_output)
    summed = base_hidden.astype(jnp.float32) + features
    nhat, rstd = norm_rows(summed)
    normed = nhat.astype(jnp.bfloat16)
    pre = jnp.dot(normed, base_up, preferred_element_type=jnp.float32)
    hidden = gelu_tanh(pre).astype(jnp.bfloat16)
    block = FF // N_TENSOR
    hidden_blocks = jnp.transpose(hidden.reshape(TOKENS, N_TENSOR, block), (1, 0, 2))
    down_blocks = jnp.transpose(base_down.reshape(D, N_TENSOR, block), (1, 0, 2))

    def add_block(carry, operands):
        hidden_block, down_block = operands
        term = lax.optimization_barrier(times_transposed(hidden_block, down_block).astype(jnp.bfloat16))
        return (carry + term.astype(jnp.float32), None)
    added, _ = lax.scan(add_block, jnp.zeros((TOKENS, D), jnp.float32), (hidden_blocks, down_blocks))
    base_out = (summed + added).astype(jnp.bfloat16)
    hidden_grad = jnp.dot(cotangent, base_down, preferred_element_type=jnp.float32)
    pre_grad = (hidden_grad * gelu_slope(pre)).astype(jnp.bfloat16)
    normed_grad = times_transposed(pre_grad, base_up)
    feat_grad = cotangent.astype(jnp.float32) + rstd * (normed_grad - lax.optimization_barrier(jnp.mean(normed_grad, axis=-1, keepdims=True)) - nhat * lax.optimization_barrier(jnp.mean(normed_grad * nhat, axis=-1, keepdims=True)))
    return (base_out, feat_grad.astype(jnp.bfloat16))
```

```python
import functools

import jax
import jax.numpy as jnp
from jax import lax
from jax.experimental import pallas as pl
from jax.experimental.pallas import tpu as pltpu
from jax.sharding import PartitionSpec as P

F32 = jnp.float32
BF16 = jnp.bfloat16
MESH = pl.DeviceIdType.MESH
D = 3072
HALF = D // 2
LANES = HALF // 2


def norm_rows(values):
    center = values - jnp.mean(values, axis=-1, keepdims=True)
    spread = jnp.mean(center * center, axis=-1, keepdims=True)
    rstd = lax.rsqrt(spread + 1e-06)
    return (center * rstd, rstd)


def head_norm(values, gain):
    square_mean = jnp.mean(values * values, axis=-1, keepdims=True)
    return (values * lax.rsqrt(square_mean + 1e-06) * gain).astype(BF16)


def times_transposed(left, right):
    return lax.dot_general(left, right, (((1,), (1,)), ((), ())), preferred_element_type=F32)


def gray(x):
    return x // 2, lax.rem((x + 1) // 2, 2) if not isinstance(x, int) else ((x + 1) // 2) % 2


class Place:
    def __init__(self):
        dp, tensor = lax.axis_index("dp"), lax.axis_index("tensor")
        self.dp, self.tensor = dp, tensor
        self.z, self.y, self.c = dp // 8, lax.rem(dp // 2, 4), lax.rem(dp, 2)
        self.w, self.x = tensor // 4, lax.rem(tensor, 4)
        self.p, self.q = gray(self.x)
        self.u, self.v = gray(self.w)
        flip = lambda i: i + 1 - 2 * lax.rem(i, 2)
        self.flip_q = (dp, self.w * 4 + flip(self.x))
        self.flip_p = (dp, self.w * 4 + 3 - self.x)
        self.flip_v = (dp, flip(self.w) * 4 + self.x)
        self.flip_u = (dp, (3 - self.w) * 4 + self.x)
        self.sibling = self.at(self.z, self.y, 1 - self.c)

    def at(self, z, y, c):
        return (z * 8 + y * 2 + c, self.tensor)

    def zs(self, j):
        return lax.rem(self.z + (j + 4), 4)

    def ys(self, j):
        return lax.rem(self.y + (j + 4), 4)

    def partners(self):
        return [self.at(self.zs(j), self.y, self.c) for j in (1, 2, 3)] + [
            self.at(self.z, self.ys(1), self.c),
            self.at(self.z, self.ys(-1), self.c),
            self.sibling,
            self.flip_q,
            self.flip_p,
            self.flip_v,
            self.flip_u,
        ]


def remote(src, dst, send, recv, device):
    return pltpu.make_async_remote_copy(
        src_ref=src, dst_ref=dst, send_sem=send, recv_sem=recv, device_id=device, device_id_type=MESH
    )


class Gather:
    def __init__(self, at, buf, send, recv):
        self.at, self.buf, self.send, self.recv = at, buf, send, recv

    def slot(self, z, y, c):
        return self.buf.at[z, y * 2 + c]

    def line(self, y, c):
        return self.buf.at[:, y * 2 + c]

    def copy(self, ref, group, sem, device):
        return remote(ref, ref, self.send.at[group], self.recv.at[sem], device)

    def wait(self, ref, sem):
        self.copy(ref, 0, sem, self.at.sibling).wait_recv()

    def both_ways(self, j):
        at = self.at
        ref = self.slot(at.zs(-j), at.y, at.c)
        self.copy(ref, 1, 3 + j, at.at(at.z, at.ys(1), at.c)).start()
        self.copy(ref, 1, 7 + j, at.at(at.z, at.ys(-1), at.c)).start()

    def start(self):
        at = self.at
        for j in (1, 2, 3):
            self.copy(self.slot(at.z, at.y, at.c), 0, j - 1, at.at(at.zs(j), at.y, at.c)).start()
        self.both_ways(0)

    def middle(self):
        at = self.at
        for j in (1, 3, 2):
            self.wait(self.slot(at.zs(-j), at.y, at.c), j - 1)
            self.both_ways(j)
        self.copy(self.line(at.y, at.c), 3, 15, at.sibling).start()

    def relay(self):
        at = self.at
        for j in (0, 1, 3, 2):
            below, above = self.slot(at.zs(-j), at.ys(-1), at.c), self.slot(at.zs(-j), at.ys(1), at.c)
            self.wait(below, 3 + j)
            if j in (0, 3):
                self.copy(below, 2, 11 + j, at.at(at.z, at.ys(1), at.c)).start()
            self.wait(above, 7 + j)
            if j in (1, 2):
                self.copy(above, 2, 11 + j, at.at(at.z, at.ys(-1), at.c)).start()
        self.copy(self.line(at.ys(-1), at.c), 3, 16, at.sibling).start()
        self.copy(self.line(at.ys(1), at.c), 3, 17, at.sibling).start()

    def finish(self):
        at = self.at
        for j in (0, 1, 3, 2):
            self.wait(self.slot(at.zs(-j), at.ys(2), at.c), 11 + j)
        self.copy(self.line(at.ys(2), at.c), 3, 18, at.sibling).start()
        for sem, step in ((15, 0), (16, -1), (17, 1), (18, 2)):
            self.wait(self.line(at.ys(step), 1 - at.c), sem)

    def drain(self):
        for group, ref in enumerate((self.buf.at[0:3, 0], self.buf.at[:, 0:2], self.buf.at[:, 0], self.buf.at[:, 0:4])):
            self.copy(ref, group, 0, self.at.sibling).wait_send()


def lanes(h):
    return pl.ds(h * LANES, LANES)


class Scatter:
    def __init__(self, at, part, r1, s1, r2, t32, t16, r3, s3, r4, send, recv):
        self.at, self.part, self.r1, self.s1, self.r2 = at, part, r1, s1, r2
        self.t32, self.t16, self.r3, self.s3, self.r4 = t32, t16, r3, s3, r4
        self.send, self.recv = send, recv

    def copies(self, level):
        at, part = self.at, self.part
        if level == 0:
            pairs = (
                (part.at[:, 1 - at.q, :, :, :, lanes(0)], self.r1.at[0], at.flip_q),
                (part.at[1 - at.p, :, :, :, :, lanes(1)], self.r1.at[1], at.flip_p),
            )
        elif level == 1:
            pairs = ((self.s1.at[0], self.r2.at[0], at.flip_p), (self.s1.at[1], self.r2.at[1], at.flip_q))
        elif level == 2:
            pairs = (
                (self.t16.at[0, :, 1 - at.v], self.r3.at[0], at.flip_v),
                (self.t16.at[1, 1 - at.u], self.r3.at[1], at.flip_u),
            )
        else:
            pairs = ((self.s3.at[0], self.r4.at[0], at.flip_u), (self.s3.at[1], self.r4.at[1], at.flip_v))
        return [
            remote(src, dst, self.send.at[2 * level + h], self.recv.at[2 * level + h], device)
            for h, (src, dst, device) in enumerate(pairs)
        ]

    def x1(self):
        for copy in self.copies(0):
            copy.start()

    def x2(self):
        at = self.at
        arrive, leave = self.copies(0), self.copies(1)
        for h, (p, q, keep) in enumerate(((1 - at.p, at.q, 1 - at.p), (at.p, 1 - at.q, 1 - at.q))):
            arrive[h].wait_recv()
            mine = self.part[p, q, :, :, :, h * LANES : (h + 1) * LANES].astype(F32)
            self.s1[h] = (mine + self.r1[h, keep].astype(F32)).astype(BF16)
            leave[h].start()

    def z1(self):
        at = self.at
        arrive, leave = self.copies(1), self.copies(2)
        for h, keep in enumerate((at.p, at.q)):
            arrive[h].wait_recv()
            mine = self.part[at.p, at.q, :, :, :, h * LANES : (h + 1) * LANES].astype(F32)
            total = mine + self.r1[h, keep].astype(F32) + self.r2[h].astype(F32)
            self.t32[h] = total
            self.t16[h] = total.astype(BF16)
            leave[h].start()

    def z2(self):
        at = self.at
        arrive, leave = self.copies(2), self.copies(3)
        for h, (u, v, keep) in enumerate(((1 - at.u, at.v, 1 - at.u), (at.u, 1 - at.v, 1 - at.v))):
            arrive[h].wait_recv()
            self.s3[h] = (self.t32[h, u, v] + self.r3[h, keep].astype(F32)).astype(BF16)
            leave[h].start()

    def done(self):
        at = self.at
        arrive = self.copies(3)
        halves = []
        for h, keep in enumerate((at.u, at.v)):
            arrive[h].wait_recv()
            halves.append(self.t32[h, at.u, at.v] + self.r3[h, keep].astype(F32) + self.r4[h].astype(F32))
        both = jnp.concatenate(halves, axis=1)
        return jnp.concatenate([both[0:8], both[8:16]], axis=1)

    def drain(self):
        for level in range(4):
            for copy in self.copies(level):
                copy.wait_send()

    def fill(self, left, matrix):
        for n in range(4):
            z, k = n // 2, 4 * (n % 2)
            depth = matrix.shape[3]
            low = times_transposed(left, matrix[z, k : k + 4].reshape(384, depth))
            high = times_transposed(left, matrix[z + 2, k : k + 4].reshape(384, depth))
            both = jnp.concatenate([low.reshape(16, 8, 384), high.reshape(16, 8, 384)], axis=1).astype(BF16)
            for t in range(16):
                (u, v), (p, q) = gray(t // 4), gray(t % 4)
                self.part[p, q, u, v, :, n * 384 : (n + 1) * 384] = both[t]


class Spread:
    def __init__(self, at, buf, send, recv):
        self.at, self.buf, self.send, self.recv = at, buf, send, recv

    def refs(self, level, h, mirror):
        at, buf = self.at, self.buf
        p, q, u, v = at.p, at.q, at.u, at.v
        everything = slice(None)
        if level == 0:
            if mirror:
                u, v = (u, 1 - v) if h == 0 else (1 - u, v)
            return buf.at[p, q, u, v, :, lanes(h)]
        if level == 1:
            if h == 0:
                return buf.at[p, q, 1 - u if mirror else u, :, :, lanes(h)]
            return buf.at[p, q, :, 1 - v if mirror else v, :, lanes(h)]
        if level == 2:
            if mirror:
                p, q = (p, 1 - q) if h == 0 else (1 - p, q)
            return buf.at[p, q, :, :, :, lanes(h)]
        if h == 0:
            return buf.at[1 - p if mirror else p, :, :, :, :, lanes(h)]
        return buf.at[:, 1 - q if mirror else q, :, :, :, lanes(h)]

    def copy(self, level, h, mirror=False):
        at = self.at
        device = ((at.flip_v, at.flip_u), (at.flip_u, at.flip_v), (at.flip_q, at.flip_p), (at.flip_p, at.flip_q))[level][h]
        ref = self.refs(level, h, mirror)
        return remote(ref, ref, self.send.at[2 * level + h], self.recv.at[2 * level + h], device)

    def step(self, level):
        for h in range(2):
            if level:
                self.copy(level - 1, h, True).wait_recv()
            if level < 4:
                self.copy(level, h).start()

    def drain(self):
        for level in range(4):
            for h in range(2):
                self.copy(level, h).wait_send()


def own_rows(ref, tensor):
    pair = ref[pl.ds(pl.multiple_of((tensor // 2) * 16, 16), 16), :].astype(F32)
    return jnp.where(lax.rem(tensor, 2) == 0, pair[0:8], pair[8:16])


def kernel(
    control_in, control_project, control_output, query_gain, key_gain, base_hidden, base_up, base_down, cotangent,
    base_out, feat_grad,
    wp_buf, kv_buf, co_buf, up_buf, down_buf, normed_in, scores, weights, spread_buf, normed, hidden_grad,
    part, r1, s1, r2, t32, t16, r3, s3, r4,
    gather_send, gather_recv, scatter_send, scatter_recv, spread_send, spread_recv,
):
    at = Place()
    barrier = pltpu.get_barrier_semaphore()
    partners = at.partners()
    for device in partners:
        pl.semaphore_signal(barrier, inc=1, device_id=device, device_id_type=MESH)

    wp, kv, co, up, down = (
        Gather(at, buf, gather_send.at[i], gather_recv.at[i])
        for i, buf in enumerate((wp_buf, kv_buf, co_buf, up_buf, down_buf))
    )
    feat, added, grad = (
        Scatter(at, *(ref.at[i] for ref in (part, r1, s1, r2, t32, t16, r3, s3, r4, scatter_send, scatter_recv)))
        for i in range(3)
    )
    spread = Spread(at, spread_buf, spread_send, spread_recv)

    yc = at.y * 2 + at.c
    for j in range(3):
        wp_buf[at.z, yc, :, j * 128 : (j + 1) * 128] = control_project[j]
    co_buf[at.z, yc] = control_output[...]
    up_buf[at.z, yc] = base_up[...]
    down_buf[at.z, yc] = base_down[...]
    pl.semaphore_wait(barrier, len(partners))

    wp.start()
    normed_in[...] = norm_rows(control_in[...].astype(F32))[0].astype(BF16)
    wp.middle()
    co.start()
    wp.relay()
    co.middle()
    wp.finish()
    projected = jnp.dot(normed_in[...], wp_buf[...].reshape(D, 384), preferred_element_type=F32)
    queries = head_norm(projected[:, 0:128], query_gain[...])
    kv_buf[at.z, yc, :, 0:128] = head_norm(projected[:, 128:256], key_gain[...])
    kv_buf[at.z, yc, :, 128:256] = projected[:, 256:384].astype(BF16)
    kv.start()
    co.relay()
    kv.middle()
    co.finish()
    kv.relay()
    up.start()
    kv.finish()
    down.start()
    for z in range(4):
        block = kv_buf[z].reshape(1024, 256)
        scores[:, z * 1024 : (z + 1) * 1024] = times_transposed(queries, block[:, 0:128]) * (1.0 / 128**0.5)
    up.middle()
    totals = []
    for r in range(4):
        rows = slice(r * 32, (r + 1) * 32)
        block = scores[rows, :]
        expo = jnp.exp(block - jnp.max(block, axis=1, keepdims=True))
        totals.append(jnp.sum(expo, axis=1, keepdims=True))
        weights[rows, :] = expo.astype(BF16)
    total = jnp.concatenate(totals, axis=0)
    accum = jnp.zeros((128, 128), F32)
    for z in range(4):
        accum = accum + jnp.dot(
            weights[:, z * 1024 : (z + 1) * 1024],
            kv_buf[z].reshape(1024, 256)[:, 128:256],
            preferred_element_type=F32,
        )
    mixed = (accum / total).astype(BF16)
    feat.fill(mixed, co_buf)
    feat.x1()
    up.relay()
    down.middle()
    feat.x2()
    feat.z1()
    up.finish()
    down.relay()
    feat.z2()
    down.finish()
    hidden_grad[...] = jnp.dot(cotangent[...], down_buf[...].reshape(D, 384), preferred_element_type=F32)
    summed = own_rows(base_hidden, at.tensor) + feat.done()
    nhat, rstd = norm_rows(summed)
    spread_buf[at.p, at.q, at.u, at.v] = jnp.concatenate([nhat[:, :HALF], nhat[:, HALF:]], axis=0).astype(BF16)
    for level in range(5):
        spread.step(level)
    for k in range(8):
        pair = []
        for t in (2 * k, 2 * k + 1):
            (u, v), (p, q) = gray(t // 4), gray(t % 4)
            pair.append(spread_buf[p, q, u, v].astype(F32))
        for h in range(2):
            normed[k * 16 : (k + 1) * 16, h * HALF : (h + 1) * HALF] = jnp.concatenate(
                [block[h * 8 : (h + 1) * 8] for block in pair], axis=0
            ).astype(BF16)
    pre = jnp.dot(normed[...], up_buf[...].reshape(D, 384), preferred_element_type=F32)
    tangent = jnp.tanh(0.7978845608028654 * (pre + 0.044715 * pre * pre * pre))
    hidden = (0.5 * pre * (1.0 + tangent)).astype(BF16)
    slope = 0.5 * (1.0 + tangent) + 0.5 * pre * (1.0 - tangent * tangent) * 0.7978845608028654 * (
        1.0 + 3.0 * 0.044715 * pre * pre
    )
    pre_grad = (hidden_grad[...] * slope).astype(BF16)
    added.fill(hidden, down_buf)
    added.x1()
    grad.fill(pre_grad, up_buf)
    grad.x1()
    added.x2()
    grad.x2()
    added.z1()
    grad.z1()
    added.z2()
    grad.z2()
    base_out[...] = summed + added.done()
    normed_grad = grad.done()
    feat_grad[...] = own_rows(cotangent, at.tensor) + rstd * (
        normed_grad
        - jnp.mean(normed_grad, axis=-1, keepdims=True)
        - nhat * jnp.mean(normed_grad * nhat, axis=-1, keepdims=True)
    )
    for each in (wp, kv, co, up, down, feat, added, grad, spread):
        each.drain()


def body(*args):
    args = list(args)
    args[3] = args[3].reshape(1, 128)
    args[4] = args[4].reshape(1, 128)
    vmem = pl.BlockSpec(memory_space=pltpu.VMEM)
    out = pl.pallas_call(
        kernel,
        out_shape=[jax.ShapeDtypeStruct((8, D), F32)] * 2,
        in_specs=[vmem] * 9,
        out_specs=[vmem] * 2,
        scratch_shapes=[
            pltpu.VMEM((4, 8, 96, 384), BF16),
            pltpu.VMEM((4, 8, 128, 256), BF16),
            pltpu.VMEM((4, 8, 96, 128), BF16),
            pltpu.VMEM((4, 8, 96, 384), BF16),
            pltpu.VMEM((4, 8, 96, 384), BF16),
            pltpu.VMEM((128, D), BF16),
            pltpu.VMEM((128, 4096), F32),
            pltpu.VMEM((128, 4096), BF16),
            pltpu.VMEM((2, 2, 2, 2, 16, HALF), BF16),
            pltpu.VMEM((128, D), BF16),
            pltpu.VMEM((128, 384), F32),
            pltpu.VMEM((3, 2, 2, 2, 2, 16, HALF), BF16),
            pltpu.VMEM((3, 2, 2, 2, 2, 16, LANES), BF16),
            pltpu.VMEM((3, 2, 2, 2, 16, LANES), BF16),
            pltpu.VMEM((3, 2, 2, 2, 16, LANES), BF16),
            pltpu.VMEM((3, 2, 2, 2, 16, LANES), F32),
            pltpu.VMEM((3, 2, 2, 2, 16, LANES), BF16),
            pltpu.VMEM((3, 2, 2, 16, LANES), BF16),
            pltpu.VMEM((3, 2, 16, LANES), BF16),
            pltpu.VMEM((3, 2, 16, LANES), BF16),
            pltpu.SemaphoreType.DMA((5, 4)),
            pltpu.SemaphoreType.DMA((5, 19)),
            pltpu.SemaphoreType.DMA((3, 8)),
            pltpu.SemaphoreType.DMA((3, 8)),
            pltpu.SemaphoreType.DMA((8,)),
            pltpu.SemaphoreType.DMA((8,)),
        ],
        compiler_params=pltpu.CompilerParams(
            collective_id=0, has_side_effects=True, vmem_limit_bytes=50 * 1024 * 1024
        ),
    )(*args)
    return tuple(each.astype(BF16) for each in out)


def solution(mesh):
    placed = (
        P("dp", None),
        P(None, "dp", "tensor"),
        P("dp", "tensor"),
        P(),
        P(),
        P("dp", None),
        P("dp", "tensor"),
        P("dp", "tensor"),
        P("dp", None),
    )
    return jax.shard_map(
        body,
        mesh=mesh,
        in_specs=placed,
        out_specs=(P(("dp", "tensor"), None), P(("dp", "tensor"), None)),
        check_vma=False,
    )
```

```python
import functools

import jax
import jax.numpy as jnp
from jax import lax
from jax.experimental import pallas as pl
from jax.experimental.pallas import tpu as pltpu
from jax.sharding import PartitionSpec as P

F32 = jnp.float32
BF16 = jnp.bfloat16
MESH = pl.DeviceIdType.MESH
D = 3072
HALF = D // 2
LANES = HALF // 2


def norm_rows(values):
    center = values - jnp.mean(values, axis=-1, keepdims=True)
    spread = jnp.mean(center * center, axis=-1, keepdims=True)
    rstd = lax.rsqrt(spread + 1e-06)
    return (center * rstd, rstd)


def head_norm(values, gain):
    square_mean = jnp.mean(values * values, axis=-1, keepdims=True)
    return (values * lax.rsqrt(square_mean + 1e-06) * gain).astype(BF16)


def times_transposed(left, right):
    return lax.dot_general(left, right, (((1,), (1,)), ((), ())), preferred_element_type=F32)


def gray(x):
    return x // 2, lax.rem((x + 1) // 2, 2) if not isinstance(x, int) else ((x + 1) // 2) % 2


class Place:
    def __init__(self):
        dp, tensor = lax.axis_index("dp"), lax.axis_index("tensor")
        self.dp, self.tensor = dp, tensor
        self.z, self.y, self.c = dp // 8, lax.rem(dp // 2, 4), lax.rem(dp, 2)
        self.w, self.x = tensor // 4, lax.rem(tensor, 4)
        self.p, self.q = gray(self.x)
        self.u, self.v = gray(self.w)
        flip = lambda i: i + 1 - 2 * lax.rem(i, 2)
        self.flip_q = (dp, self.w * 4 + flip(self.x))
        self.flip_p = (dp, self.w * 4 + 3 - self.x)
        self.flip_v = (dp, flip(self.w) * 4 + self.x)
        self.flip_u = (dp, (3 - self.w) * 4 + self.x)
        self.sibling = self.at(self.z, self.y, 1 - self.c)

    def at(self, z, y, c):
        return (z * 8 + y * 2 + c, self.tensor)

    def zs(self, j):
        return lax.rem(self.z + (j + 4), 4)

    def ys(self, j):
        return lax.rem(self.y + (j + 4), 4)

    def xs(self, j):
        return lax.rem(self.x + (j + 4), 4)

    def ws(self, j):
        return lax.rem(self.w + (j + 4), 4)

    def tensor_at(self, w, x):
        return (self.dp, w * 4 + x)

    def partners(self):
        return (
            [self.at(self.zs(j), self.y, self.c) for j in (1, 2, 3)]
            + [self.at(self.z, self.ys(j), self.c) for j in (1, -1)]
            + [self.sibling]
            + self.x_peers()
            + self.w_peers()
        )

    def x_peers(self):
        return [self.tensor_at(self.w, self.xs(j)) for j in (1, 2, 3)]

    def w_peers(self):
        return [self.tensor_at(self.ws(j), self.x) for j in (1, 2, 3)]


def remote(src, dst, send, recv, device):
    return pltpu.make_async_remote_copy(
        src_ref=src, dst_ref=dst, send_sem=send, recv_sem=recv, device_id=device, device_id_type=MESH
    )


class Gather:
    def __init__(self, at, buf, send, recv):
        self.at, self.buf, self.send, self.recv = at, buf, send, recv

    def slot(self, z, y, c):
        return self.buf.at[z, y, c]

    def line(self, y, c):
        return self.buf.at[:, y, c]

    def copy(self, ref, group, sem, device):
        return remote(ref, ref, self.send.at[group], self.recv.at[sem], device)

    def wait(self, ref, sem):
        self.copy(ref, 0, sem, self.at.sibling).wait_recv()

    def both_ways(self, j):
        at = self.at
        ref = self.slot(at.zs(-j), at.y, at.c)
        self.copy(ref, 1, 3 + j, at.at(at.z, at.ys(1), at.c)).start()
        self.copy(ref, 1, 7 + j, at.at(at.z, at.ys(-1), at.c)).start()

    def start(self):
        at = self.at
        for j in (1, 3, 2):
            self.copy(self.slot(at.z, at.y, at.c), 0, j - 1, at.at(at.zs(j), at.y, at.c)).start()
        self.both_ways(0)

    def middle(self):
        at = self.at
        for j in (1, 3, 2):
            self.wait(self.slot(at.zs(-j), at.y, at.c), j - 1)
            self.both_ways(j)
        self.copy(self.line(at.y, at.c), 3, 15, at.sibling).start()

    def relay(self):
        at = self.at
        for j in (0, 1, 3, 2):
            below, above = self.slot(at.zs(-j), at.ys(-1), at.c), self.slot(at.zs(-j), at.ys(1), at.c)
            self.wait(below, 3 + j)
            if j in (0, 3):
                self.copy(below, 2, 11 + j, at.at(at.z, at.ys(1), at.c)).start()
            self.wait(above, 7 + j)
            if j in (1, 2):
                self.copy(above, 2, 11 + j, at.at(at.z, at.ys(-1), at.c)).start()
        self.copy(self.line(at.ys(-1), at.c), 3, 16, at.sibling).start()
        self.copy(self.line(at.ys(1), at.c), 3, 17, at.sibling).start()

    def finish(self):
        at = self.at
        for j in (0, 1, 3, 2):
            self.wait(self.slot(at.zs(-j), at.ys(2), at.c), 11 + j)
        self.copy(self.line(at.ys(2), at.c), 3, 18, at.sibling).start()

    def settle(self):
        at = self.at
        for sem, step in ((15, 0), (16, -1), (17, 1), (18, 2)):
            self.wait(self.line(at.ys(step), 1 - at.c), sem)

    def drain(self):
        buf = self.buf
        for group, ref in enumerate((buf.at[0:3, 0, 0], buf.at[:, 0], buf.at[:, 0, 0], buf.at[:, :, 0])):
            self.copy(ref, group, 0, self.at.sibling).wait_send()


class Across:
    def __init__(self, at, buf, send, recv):
        self.at, self.buf, self.send, self.recv = at, buf, send, recv

    def line(self, x, step):
        return self.buf.at[x, :, self.at.ys(step), self.at.c]

    def copy(self, ref, group, sem, device):
        return remote(ref, ref, self.send.at[group], self.recv.at[sem], device)

    def start(self, *steps):
        at = self.at
        for step in steps:
            for i in (1, 3, 2):
                self.copy(self.line(at.x, step), 0, (step + 1) * 3 + i - 1, at.tensor_at(at.w, at.xs(i))).start()

    def swap(self):
        at = self.at
        for i in (1, 3, 2):
            for step in (0, -1, 1, 2):
                self.copy(self.line(at.xs(-i), step), 0, (step + 1) * 3 + i - 1, at.sibling).wait_recv()
            self.copy(self.buf.at[at.xs(-i), :, :, at.c], 1, 12 + i - 1, at.sibling).start()

    def settle(self):
        at = self.at
        for i in (1, 3, 2):
            self.copy(self.buf.at[at.xs(-i), :, :, 1 - at.c], 1, 12 + i - 1, at.sibling).wait_recv()

    def drain(self):
        for group in range(2):
            self.copy(self.buf.at[0:3, :, :, 0], group, 0, self.at.sibling).wait_send()


def lanes(h):
    return pl.ds(h * LANES, LANES)


class Scatter:
    def __init__(self, at, part, r1, s1, r2, t32, t16, r3, s3, r4, send, recv):
        self.at, self.part, self.r1, self.s1, self.r2 = at, part, r1, s1, r2
        self.t32, self.t16, self.r3, self.s3, self.r4 = t32, t16, r3, s3, r4
        self.send, self.recv = send, recv

    def copies(self, level):
        at, part = self.at, self.part
        if level == 0:
            pairs = (
                (part.at[:, 1 - at.q, :, :, :, lanes(0)], self.r1.at[0], at.flip_q),
                (part.at[1 - at.p, :, :, :, :, lanes(1)], self.r1.at[1], at.flip_p),
            )
        elif level == 1:
            pairs = ((self.s1.at[0], self.r2.at[0], at.flip_p), (self.s1.at[1], self.r2.at[1], at.flip_q))
        elif level == 2:
            pairs = (
                (self.t16.at[0, :, 1 - at.v], self.r3.at[0], at.flip_v),
                (self.t16.at[1, 1 - at.u], self.r3.at[1], at.flip_u),
            )
        else:
            pairs = ((self.s3.at[0], self.r4.at[0], at.flip_u), (self.s3.at[1], self.r4.at[1], at.flip_v))
        return [
            remote(src, dst, self.send.at[2 * level + h], self.recv.at[2 * level + h], device)
            for h, (src, dst, device) in enumerate(pairs)
        ]

    def x1(self):
        for copy in self.copies(0):
            copy.start()

    def x2(self):
        at = self.at
        arrive, leave = self.copies(0), self.copies(1)
        for h, (p, q, keep) in enumerate(((1 - at.p, at.q, 1 - at.p), (at.p, 1 - at.q, 1 - at.q))):
            arrive[h].wait_recv()
            mine = self.part[p, q, :, :, :, h * LANES : (h + 1) * LANES].astype(F32)
            self.s1[h] = (mine + self.r1[h, keep].astype(F32)).astype(BF16)
            leave[h].start()

    def z1(self):
        at = self.at
        arrive, leave = self.copies(1), self.copies(2)
        for h, keep in enumerate((at.p, at.q)):
            arrive[h].wait_recv()
            mine = self.part[at.p, at.q, :, :, :, h * LANES : (h + 1) * LANES].astype(F32)
            total = mine + self.r1[h, keep].astype(F32) + self.r2[h].astype(F32)
            self.t32[h] = total
            self.t16[h] = total.astype(BF16)
            leave[h].start()

    def z2(self):
        at = self.at
        arrive, leave = self.copies(2), self.copies(3)
        for h, (u, v, keep) in enumerate(((1 - at.u, at.v, 1 - at.u), (at.u, 1 - at.v, 1 - at.v))):
            arrive[h].wait_recv()
            self.s3[h] = (self.t32[h, u, v] + self.r3[h, keep].astype(F32)).astype(BF16)
            leave[h].start()

    def done(self):
        at = self.at
        arrive = self.copies(3)
        halves = []
        for h, keep in enumerate((at.u, at.v)):
            arrive[h].wait_recv()
            halves.append(self.t32[h, at.u, at.v] + self.r3[h, keep].astype(F32) + self.r4[h].astype(F32))
        both = jnp.concatenate(halves, axis=1)
        return jnp.concatenate([both[0:8], both[8:16]], axis=1)

    def drain(self):
        for level in range(4):
            for copy in self.copies(level):
                copy.wait_send()

    def fill(self, left, matrix):
        for n in range(4):
            low = times_transposed(left, row_block(matrix, n))
            high = times_transposed(left, row_block(matrix, n + 4))
            both = jnp.concatenate([low.reshape(16, 8, 384), high.reshape(16, 8, 384)], axis=1).astype(BF16)
            for t in range(16):
                (u, v), (p, q) = gray(t // 4), gray(t % 4)
                self.part[p, q, u, v, :, n * 384 : (n + 1) * 384] = both[t]


class Direct:
    def __init__(self, send, recv, peers):
        self.send, self.recv, self.peers = send, recv, peers

    def copy(self, j, src, dst):
        return remote(src, dst, self.send.at[j - 1], self.recv.at[j - 1], self.peers[j - 1])


class Spread:
    def __init__(self, at, buf, send, recv):
        self.at, self.buf, self.send, self.recv = at, buf, send, recv

    def copy(self, ref, group, sem, device):
        return remote(ref, ref, self.send.at[group], self.recv.at[sem], device)

    def along_x(self, j):
        at = self.at
        for i in (1, 3, 2):
            self.copy(self.buf.at[at.ws(-j), at.x], 1, 3 + 3 * j + i - 1, at.tensor_at(at.w, at.xs(i))).start()

    def start(self):
        at = self.at
        for j in (2, 1, 3):
            self.copy(self.buf.at[at.w, at.x], 0, j - 1, at.tensor_at(at.ws(j), at.x)).start()
        self.along_x(0)

    def finish(self):
        at = self.at
        for j in (1, 3, 2):
            self.copy(self.buf.at[at.ws(-j), at.x], 0, j - 1, at.sibling).wait_recv()
            self.along_x(j)
        for j in (0, 1, 3, 2):
            for i in (1, 3, 2):
                self.copy(self.buf.at[at.ws(-j), at.xs(-i)], 1, 3 + 3 * j + i - 1, at.sibling).wait_recv()

    def drain(self):
        self.copy(self.buf.at[0:3, 0], 0, 0, self.at.sibling).wait_send()
        self.copy(self.buf.at[0:3], 1, 0, self.at.sibling).wait_send()


def row_block(matrix, n):
    y = 2 * (n % 2)
    return matrix[n // 2, y : y + 2].reshape(384, matrix.shape[-1])


def row_pair(ref, tensor):
    return ref.at[pl.ds(pl.multiple_of((tensor // 2) * 16, 16), 16), :]


def own_rows(pair, tensor):
    pair = pair.astype(F32)
    return jnp.where(lax.rem(tensor, 2) == 0, pair[0:8], pair[8:16])


def kernel(
    control_in, control_project, control_output, query_gain, key_gain, base_hidden, base_up, base_down, cotangent,
    base_out, feat_grad,
    w_buf, k_buf, v_buf, co_buf, up_buf, down_buf, own_in, own_gain, own_base, own_cot,
    normed_in, scores, weights, mix_send, mix_recv, feat32, feat16, feat_recv, spread_buf, normed, hidden_grad,
    part, r1, s1, r2, t32, t16, r3, s3, r4,
    local_sem, gather_send, gather_recv, across_send, across_recv, direct_send, direct_recv,
    scatter_send, scatter_recv, spread_send, spread_recv,
):
    at = Place()
    barrier = pltpu.get_barrier_semaphore()
    partners = at.partners()
    for device in partners:
        pl.semaphore_signal(barrier, inc=1, device_id=device, device_id_type=MESH)

    wq, wk, wv, ks, vs, co, up, down = (
        Gather(at, buf, gather_send.at[i], gather_recv.at[i])
        for i, buf in enumerate(
            (w_buf.at[0], w_buf.at[1], w_buf.at[2], k_buf, v_buf, co_buf.at[at.x], up_buf, down_buf)
        )
    )
    co_x = Across(at, co_buf, across_send, across_recv)
    added, grad = (
        Scatter(at, *(ref.at[i] for ref in (part, r1, s1, r2, t32, t16, r3, s3, r4, scatter_send, scatter_recv)))
        for i in range(2)
    )
    spread = Spread(at, spread_buf, spread_send, spread_recv)
    heads = Direct(direct_send.at[0], direct_recv.at[0], at.x_peers())
    feats = Direct(direct_send.at[1], direct_recv.at[1], at.w_peers())

    def own(gather):
        return gather.slot(at.z, at.y, at.c)

    loads = [
        pltpu.make_async_copy(src, dst, local_sem.at[i])
        for i, (src, dst) in enumerate(
            (
                (control_project.at[1], own(wk)),
                (control_project.at[2], own(wv)),
                (control_project.at[0], own(wq)),
                (control_in, own_in),
                (control_output, own(co)),
                (query_gain, own_gain.at[0]),
                (key_gain, own_gain.at[1]),
                (base_up, own(up)),
                (base_down, own(down)),
                (row_pair(base_hidden, at.tensor), own_base),
                (cotangent, own_cot),
            )
        )
    ]
    for load in loads:
        load.start()
    pl.semaphore_wait(barrier, len(partners))

    for load, gather in zip(loads, (wk, wv, wq)):
        load.wait()
        gather.start()
    loads[3].wait()
    normed_in[...] = norm_rows(own_in[...].astype(F32))[0].astype(BF16)
    loads[4].wait()
    wk.middle()
    wv.middle()
    wq.middle()
    co.start()
    wk.relay()
    wv.relay()
    wk.finish()
    wq.relay()
    wv.finish()
    co.middle()
    co_x.start(0)
    for load in loads[5:]:
        load.wait()
    wk.settle()
    keys = jnp.dot(normed_in[...], w_buf[1].reshape(D, 128), preferred_element_type=F32)
    k_buf[at.z, at.y, at.c] = head_norm(keys, own_gain[1])
    ks.start()
    wv.settle()
    values = jnp.dot(normed_in[...], w_buf[2].reshape(D, 128), preferred_element_type=F32)
    v_buf[at.z, at.y, at.c] = values.astype(BF16)
    vs.start()
    wq.finish()
    co.relay()
    co_x.start(-1, 1)
    ks.middle()
    wq.settle()
    queries = head_norm(
        jnp.dot(normed_in[...], w_buf[0].reshape(D, 128), preferred_element_type=F32), own_gain[0]
    )
    vs.middle()
    co.finish()
    co_x.start(2)
    ks.relay()
    vs.relay()
    up.start()
    ks.finish()
    vs.finish()
    down.start()
    co.settle()
    ks.settle()
    for z in range(4):
        block = k_buf[z].reshape(1024, 128)
        scores[:, z * 1024 : (z + 1) * 1024] = times_transposed(queries, block) * (1.0 / 128**0.5)
    co_x.swap()
    totals = []
    for r in range(4):
        rows = slice(r * 32, (r + 1) * 32)
        block = scores[rows, :]
        expo = jnp.exp(block - jnp.max(block, axis=1, keepdims=True))
        totals.append(jnp.sum(expo, axis=1, keepdims=True))
        weights[rows, :] = expo.astype(BF16)
    total = jnp.concatenate(totals, axis=0)
    vs.settle()
    accum = jnp.zeros((128, 128), F32)
    for z in range(4):
        accum = accum + jnp.dot(
            weights[:, z * 1024 : (z + 1) * 1024], v_buf[z].reshape(1024, 128), preferred_element_type=F32
        )
    mixed = (accum / total).reshape(4, 4, 8, 128)
    for x in range(4):
        mix_send[x] = mixed[:, x].reshape(32, 128).astype(BF16)
    for j in (1, 3, 2):
        heads.copy(j, mix_send.at[at.xs(j)], mix_recv.at[at.x]).start()
    mix_recv[at.x] = mix_send[at.x]
    up.middle()
    co_x.settle()
    for j in (1, 3, 2):
        heads.copy(j, mix_send.at[at.xs(j)], mix_recv.at[at.xs(-j)]).wait_recv()
    mixed = jnp.concatenate([mix_recv[x] for x in range(4)], axis=1)
    for n in range(4):
        low, high = (
            times_transposed(
                mixed, jnp.concatenate([row_block(co_buf.at[x], m) for x in range(4)], axis=1)
            ).reshape(4, 8, 384)
            for m in (n, n + 4)
        )
        both = jnp.concatenate([low, high], axis=1)
        feat32[:, :, n * 384 : (n + 1) * 384] = both
        feat16[:, :, n * 384 : (n + 1) * 384] = both.astype(BF16)
    for j in (2, 1, 3):
        feats.copy(j, feat16.at[at.ws(j)], feat_recv.at[j - 1]).start()
    down.middle()
    up.relay()
    down.relay()
    up.finish()
    down.finish()
    feat = feat32[at.w]
    for j in (1, 3, 2):
        feats.copy(j, feat16.at[at.ws(j)], feat_recv.at[j - 1]).wait_recv()
        feat = feat + feat_recv[j - 1].astype(F32)
    summed = own_rows(own_base[...], at.tensor) + jnp.concatenate([feat[0:8], feat[8:16]], axis=1)
    nhat, rstd = norm_rows(summed)
    spread_buf[at.w, at.x] = jnp.concatenate([nhat[:, :HALF], nhat[:, HALF:]], axis=0).astype(BF16)
    spread.start()
    up.settle()
    down.settle()
    hidden_grad[...] = jnp.dot(own_cot[...], down_buf[...].reshape(D, 384), preferred_element_type=F32)
    spread.finish()
    for k in range(8):
        pair = [spread_buf[t // 4, t % 4].astype(F32) for t in (2 * k, 2 * k + 1)]
        for h in range(2):
            normed[k * 16 : (k + 1) * 16, h * HALF : (h + 1) * HALF] = jnp.concatenate(
                [block[h * 8 : (h + 1) * 8] for block in pair], axis=0
            ).astype(BF16)
    pre = jnp.dot(normed[...], up_buf[...].reshape(D, 384), preferred_element_type=F32)
    tangent = jnp.tanh(0.7978845608028654 * (pre + 0.044715 * pre * pre * pre))
    hidden = (0.5 * pre * (1.0 + tangent)).astype(BF16)
    slope = 0.5 * (1.0 + tangent) + 0.5 * pre * (1.0 - tangent * tangent) * 0.7978845608028654 * (
        1.0 + 3.0 * 0.044715 * pre * pre
    )
    pre_grad = (hidden_grad[...] * slope).astype(BF16)
    added.fill(hidden, down_buf)
    added.x1()
    grad.fill(pre_grad, up_buf)
    grad.x1()
    added.x2()
    grad.x2()
    added.z1()
    grad.z1()
    added.z2()
    grad.z2()
    base_out[...] = summed + added.done()
    normed_grad = grad.done()
    feat_grad[...] = own_rows(row_pair(own_cot, at.tensor)[...], at.tensor) + rstd * (
        normed_grad
        - jnp.mean(normed_grad, axis=-1, keepdims=True)
        - nhat * jnp.mean(normed_grad * nhat, axis=-1, keepdims=True)
    )
    for each in (wq, wk, wv, ks, vs, co, up, down, co_x, spread, added, grad):
        each.drain()
    for j in (1, 2, 3):
        heads.copy(j, mix_send.at[at.xs(j)], mix_recv.at[at.x]).wait_send()
        feats.copy(j, feat16.at[at.ws(j)], feat_recv.at[j - 1]).wait_send()


def body(*args):
    args = list(args)
    args[3] = args[3].reshape(1, 128)
    args[4] = args[4].reshape(1, 128)
    vmem = pl.BlockSpec(memory_space=pltpu.VMEM)
    out = pl.pallas_call(
        kernel,
        out_shape=[jax.ShapeDtypeStruct((8, D), F32)] * 2,
        in_specs=[pl.BlockSpec(memory_space=pltpu.HBM)] * 9,
        out_specs=[vmem] * 2,
        scratch_shapes=[
            pltpu.VMEM((3, 4, 4, 2, 96, 128), BF16),
            pltpu.VMEM((4, 4, 2, 128, 128), BF16),
            pltpu.VMEM((4, 4, 2, 128, 128), BF16),
            pltpu.VMEM((4, 4, 4, 2, 96, 128), BF16),
            pltpu.VMEM((4, 4, 2, 96, 384), BF16),
            pltpu.VMEM((4, 4, 2, 96, 384), BF16),
            pltpu.VMEM((128, D), BF16),
            pltpu.VMEM((2, 1, 128), F32),
            pltpu.VMEM((16, D), BF16),
            pltpu.VMEM((128, D), BF16),
            pltpu.VMEM((128, D), BF16),
            pltpu.VMEM((128, 4096), F32),
            pltpu.VMEM((128, 4096), BF16),
            pltpu.VMEM((4, 32, 128), BF16),
            pltpu.VMEM((4, 32, 128), BF16),
            pltpu.VMEM((4, 16, HALF), F32),
            pltpu.VMEM((4, 16, HALF), BF16),
            pltpu.VMEM((3, 16, HALF), BF16),
            pltpu.VMEM((4, 4, 16, HALF), BF16),
            pltpu.VMEM((128, D), BF16),
            pltpu.VMEM((128, 384), F32),
            pltpu.VMEM((2, 2, 2, 2, 2, 16, HALF), BF16),
            pltpu.VMEM((2, 2, 2, 2, 2, 16, LANES), BF16),
            pltpu.VMEM((2, 2, 2, 2, 16, LANES), BF16),
            pltpu.VMEM((2, 2, 2, 2, 16, LANES), BF16),
            pltpu.VMEM((2, 2, 2, 2, 16, LANES), F32),
            pltpu.VMEM((2, 2, 2, 2, 16, LANES), BF16),
            pltpu.VMEM((2, 2, 2, 16, LANES), BF16),
            pltpu.VMEM((2, 2, 16, LANES), BF16),
            pltpu.VMEM((2, 2, 16, LANES), BF16),
            pltpu.SemaphoreType.DMA((11,)),
            pltpu.SemaphoreType.DMA((8, 4)),
            pltpu.SemaphoreType.DMA((8, 19)),
            pltpu.SemaphoreType.DMA((2,)),
            pltpu.SemaphoreType.DMA((15,)),
            pltpu.SemaphoreType.DMA((2, 3)),
            pltpu.SemaphoreType.DMA((2, 3)),
            pltpu.SemaphoreType.DMA((2, 8)),
            pltpu.SemaphoreType.DMA((2, 8)),
            pltpu.SemaphoreType.DMA((2,)),
            pltpu.SemaphoreType.DMA((15,)),
        ],
        compiler_params=pltpu.CompilerParams(
            collective_id=0, has_side_effects=True, vmem_limit_bytes=64000 * 1024
        ),
    )(*args)
    return tuple(each.astype(BF16) for each in out)


def solution(mesh):
    placed = (
        P("dp", None),
        P(None, "dp", "tensor"),
        P("dp", "tensor"),
        P(),
        P(),
        P("dp", None),
        P("dp", "tensor"),
        P("dp", "tensor"),
        P("dp", None),
    )
    return jax.shard_map(
        body,
        mesh=mesh,
        in_specs=placed,
        out_specs=(P(("dp", "tensor"), None), P(("dp", "tensor"), None)),
        check_vma=False,
    )
```

```python
import functools

import jax
import jax.numpy as jnp
from jax import lax
from jax.experimental import pallas as pl
from jax.experimental.pallas import tpu as pltpu
from jax.sharding import PartitionSpec as P

F32 = jnp.float32
BF16 = jnp.bfloat16
MESH = pl.DeviceIdType.MESH
D = 3072
HALF = D // 2


def norm_rows(values):
    center = values - jnp.mean(values, axis=-1, keepdims=True)
    spread = jnp.mean(center * center, axis=-1, keepdims=True)
    rstd = lax.rsqrt(spread + 1e-06)
    return (center * rstd, rstd)


def head_norm(values, gain):
    square_mean = jnp.mean(values * values, axis=-1, keepdims=True)
    return (values * lax.rsqrt(square_mean + 1e-06) * gain).astype(BF16)


def times_transposed(left, right):
    return lax.dot_general(left, right, (((1,), (1,)), ((), ())), preferred_element_type=F32)


class Place:
    def __init__(self):
        dp, tensor = lax.axis_index("dp"), lax.axis_index("tensor")
        self.dp, self.tensor = dp, tensor
        self.z, self.y, self.c = dp // 8, lax.rem(dp // 2, 4), lax.rem(dp, 2)
        self.w, self.x = tensor // 4, lax.rem(tensor, 4)
        self.sibling = self.at(self.z, self.y, 1 - self.c)

    def at(self, z, y, c):
        return (z * 8 + y * 2 + c, self.tensor)

    def zs(self, j):
        return lax.rem(self.z + (j + 4), 4)

    def ys(self, j):
        return lax.rem(self.y + (j + 4), 4)

    def xs(self, j):
        return lax.rem(self.x + (j + 4), 4)

    def ws(self, j):
        return lax.rem(self.w + (j + 4), 4)

    def tensor_at(self, w, x):
        return (self.dp, w * 4 + x)

    def partners(self):
        return (
            self.z_peers()
            + self.y_peers()
            + [self.sibling]
            + self.x_peers()
            + self.w_peers()
        )

    def z_peers(self):
        return [self.at(self.zs(j), self.y, self.c) for j in (1, 2, 3)]

    def y_peers(self):
        return [self.at(self.z, self.ys(j), self.c) for j in (1, 2, 3)]

    def x_peers(self):
        return [self.tensor_at(self.w, self.xs(j)) for j in (1, 2, 3)]

    def w_peers(self):
        return [self.tensor_at(self.ws(j), self.x) for j in (1, 2, 3)]


def remote(src, dst, send, recv, device):
    return pltpu.make_async_remote_copy(
        src_ref=src, dst_ref=dst, send_sem=send, recv_sem=recv, device_id=device, device_id_type=MESH
    )


class Gather:
    def __init__(self, at, buf, send, recv):
        self.at, self.buf, self.send, self.recv = at, buf, send, recv

    def slot(self, z, y, c):
        return self.buf.at[z, y, c]

    def line(self, y, c):
        return self.buf.at[:, y, c]

    def copy(self, ref, group, sem, device):
        return remote(ref, ref, self.send.at[group], self.recv.at[sem], device)

    def wait(self, ref, sem):
        self.copy(ref, 0, sem, self.at.sibling).wait_recv()

    def both_ways(self, j):
        at = self.at
        ref = self.slot(at.zs(-j), at.y, at.c)
        self.copy(ref, 1, 3 + j, at.at(at.z, at.ys(1), at.c)).start()
        self.copy(ref, 1, 7 + j, at.at(at.z, at.ys(-1), at.c)).start()

    def start(self):
        at = self.at
        for j in (1, 3, 2):
            self.copy(self.slot(at.z, at.y, at.c), 0, j - 1, at.at(at.zs(j), at.y, at.c)).start()

    def middle(self, own=True):
        at = self.at
        if own:
            self.both_ways(0)
        for j in (1, 3, 2):
            self.wait(self.slot(at.zs(-j), at.y, at.c), j - 1)
            self.both_ways(j)
        self.copy(self.line(at.y, at.c), 3, 15, at.sibling).start()

    def relay(self):
        at = self.at
        for j in (0, 1, 3, 2):
            below, above = self.slot(at.zs(-j), at.ys(-1), at.c), self.slot(at.zs(-j), at.ys(1), at.c)
            self.wait(below, 3 + j)
            if j in (0, 3):
                self.copy(below, 2, 11 + j, at.at(at.z, at.ys(1), at.c)).start()
            self.wait(above, 7 + j)
            if j in (1, 2):
                self.copy(above, 2, 11 + j, at.at(at.z, at.ys(-1), at.c)).start()
        self.copy(self.line(at.ys(-1), at.c), 3, 16, at.sibling).start()
        self.copy(self.line(at.ys(1), at.c), 3, 17, at.sibling).start()

    def finish(self):
        at = self.at
        for j in (0, 1, 3, 2):
            self.wait(self.slot(at.zs(-j), at.ys(2), at.c), 11 + j)
        self.copy(self.line(at.ys(2), at.c), 3, 18, at.sibling).start()

    def settle(self):
        at = self.at
        for sem, step in ((15, 0), (16, -1), (17, 1), (18, 2)):
            self.wait(self.line(at.ys(step), 1 - at.c), sem)

    def drain(self):
        buf = self.buf
        for group, ref in enumerate((buf.at[0:3, 0, 0], buf.at[:, 0], buf.at[:, 0, 0], buf.at[:, :, 0])):
            self.copy(ref, group, 0, self.at.sibling).wait_send()


class Across:
    def __init__(self, at, buf, send, recv):
        self.at, self.buf, self.send, self.recv = at, buf, send, recv

    def line(self, x, step):
        return self.buf.at[x, :, self.at.ys(step), self.at.c]

    def copy(self, ref, group, sem, device):
        return remote(ref, ref, self.send.at[group], self.recv.at[sem], device)

    def start(self, *steps):
        at = self.at
        for step in steps:
            for i in (1, 3, 2):
                self.copy(self.line(at.x, step), 0, (step + 1) * 3 + i - 1, at.tensor_at(at.w, at.xs(i))).start()

    def swap(self):
        at = self.at
        for i in (1, 3, 2):
            for step in (0, -1, 1, 2):
                self.copy(self.line(at.xs(-i), step), 0, (step + 1) * 3 + i - 1, at.sibling).wait_recv()
            self.copy(self.buf.at[at.xs(-i), :, :, at.c], 1, 12 + i - 1, at.sibling).start()

    def settle(self):
        at = self.at
        for i in (1, 3, 2):
            self.copy(self.buf.at[at.xs(-i), :, :, 1 - at.c], 1, 12 + i - 1, at.sibling).wait_recv()

    def drain(self):
        for group in range(2):
            self.copy(self.buf.at[0:3, :, :, 0], group, 0, self.at.sibling).wait_send()


class Scatter:
    def __init__(self, at, part, from_x, total, from_w, x_send, x_recv, w_send, w_recv):
        self.at, self.part, self.from_x, self.total, self.from_w = at, part, from_x, total, from_w
        self.x_send, self.x_recv, self.w_send, self.w_recv = x_send, x_recv, w_send, w_recv

    def x_copy(self, j, i):
        at = self.at
        return remote(
            self.part.at[j, at.xs(i)], self.from_x.at[j, i - 1], self.x_send, self.x_recv.at[3 * j + i - 1],
            at.tensor_at(at.w, at.xs(i)),
        )

    def w_copy(self, j):
        at = self.at
        return remote(
            self.total.at[j - 1], self.from_w.at[j - 1], self.w_send, self.w_recv.at[j - 1],
            at.tensor_at(at.ws(-j), at.x),
        )

    def fill(self, groups, left, matrix):
        for n in range(4):
            low, high = (
                times_transposed(left, row_block(matrix, m)).reshape(4 * len(groups), 8, 384) for m in (n, n + 4)
            )
            both = jnp.concatenate([low, high], axis=1).astype(BF16)
            for k, j in enumerate(groups):
                for x in range(4):
                    self.part[j, x, :, n * 384 : (n + 1) * 384] = both[4 * k + x]
        for j in groups:
            for i in (1, 3, 2):
                self.x_copy(j, i).start()

    def sum_x(self, j):
        total = self.part[j, self.at.x].astype(F32)
        for i in (1, 3, 2):
            self.x_copy(j, i).wait_recv()
            total = total + self.from_x[j, i - 1].astype(F32)
        return total

    def pass_on(self, j):
        self.total[j - 1] = self.sum_x(j).astype(BF16)
        self.w_copy(j).start()

    def done(self):
        total = self.sum_x(0)
        for j in (1, 3, 2):
            self.w_copy(j).wait_recv()
            total = total + self.from_w[j - 1].astype(F32)
        return jnp.concatenate([total[0:8], total[8:16]], axis=1)

    def drain(self):
        at = self.at
        whole = self.part.at[0:3]
        remote(whole, whole, self.x_send, self.x_recv.at[0], at.sibling).wait_send()
        remote(self.total, self.total, self.w_send, self.w_recv.at[0], at.sibling).wait_send()


class Direct:
    def __init__(self, send, recv, peers):
        self.send, self.recv, self.peers = send, recv, peers

    def copy(self, j, src, dst):
        return remote(src, dst, self.send.at[j - 1], self.recv.at[j - 1], self.peers[j - 1])


class Lines:
    def __init__(self, at, buf, send, recv):
        self.at, self.buf, self.send, self.recv = at, buf, send, recv

    def copy(self, i, other=False):
        at = self.at
        ref = self.buf.at[at.ys(-i), 1 - at.c if other else at.c]
        return remote(ref, ref, self.send.at[3 + i], self.recv.at[3 + i], at.sibling)

    def along_y(self, i):
        at = self.at
        ref = self.buf.at[at.y, at.c]
        return remote(ref, ref, self.send.at[i - 1], self.recv.at[i - 1], at.y_peers()[i - 1])

    def start(self):
        for i in (2, 1, 3):
            self.along_y(i).start()
        self.copy(0).start()

    def middle(self):
        at = self.at
        for i in (1, 3, 2):
            ref = self.buf.at[at.ys(-i), at.c]
            remote(ref, ref, self.send.at[i - 1], self.recv.at[i - 1], at.sibling).wait_recv()
            self.copy(i).start()

    def settle(self):
        for i in (0, 1, 3, 2):
            self.copy(i, True).wait_recv()

    def drain(self):
        for i in (1, 2, 3):
            self.along_y(i).wait_send()
        for i in range(4):
            self.copy(i).wait_send()


class Spread:
    def __init__(self, at, buf, send, recv):
        self.at, self.buf, self.send, self.recv = at, buf, send, recv

    def copy(self, ref, group, sem, device):
        return remote(ref, ref, self.send.at[group], self.recv.at[sem], device)

    def along_x(self, j):
        at = self.at
        for i in (1, 3, 2):
            self.copy(self.buf.at[at.ws(-j), at.x], 1, 3 + 3 * j + i - 1, at.tensor_at(at.w, at.xs(i))).start()

    def start(self):
        at = self.at
        for j in (1, 3, 2):
            self.copy(self.buf.at[at.w, at.x], 0, j - 1, at.tensor_at(at.ws(j), at.x)).start()
        self.along_x(0)

    def forward(self, j):
        at = self.at
        self.copy(self.buf.at[at.ws(-j), at.x], 0, j - 1, at.sibling).wait_recv()
        self.along_x(j)

    def settle(self, j):
        at = self.at
        for i in (1, 3, 2):
            self.copy(self.buf.at[at.ws(-j), at.xs(-i)], 1, 3 + 3 * j + i - 1, at.sibling).wait_recv()

    def drain(self):
        self.copy(self.buf.at[0:3, 0], 0, 0, self.at.sibling).wait_send()
        self.copy(self.buf.at[0:3], 1, 0, self.at.sibling).wait_send()


def row_block(matrix, n):
    y = 2 * (n % 2)
    return matrix[n // 2, y : y + 2].reshape(384, matrix.shape[-1])


def row_pair(ref, tensor):
    return ref.at[pl.ds(pl.multiple_of((tensor // 2) * 16, 16), 16), :]


def own_rows(pair, tensor):
    pair = pair.astype(F32)
    return jnp.where(lax.rem(tensor, 2) == 0, pair[0:8], pair[8:16])


def kernel(
    control_in, control_project, control_output, query_gain, key_gain, base_hidden, base_up, base_down, cotangent,
    base_out, feat_grad,
    w_buf, kv_buf, q_buf, co_buf, up_buf, down_buf, own_in, own_gain, own_base, own_cot,
    normed_in, scores, stat, stat_back, mix32, mix16, mix_back, mix_send, mix_recv, feat32, feat16, feat_recv, spread_buf, normed, hidden_grad,
    part, from_x, total, from_w,
    local_sem, gather_send, gather_recv, kv_send, kv_recv, across_send, across_recv, direct_send, direct_recv,
    x_send, x_recv, w_send, w_recv, spread_send, spread_recv,
):
    at = Place()
    barrier = pltpu.get_barrier_semaphore()
    partners = at.partners()
    for device in partners:
        pl.semaphore_signal(barrier, inc=1, device_id=device, device_id_type=MESH)

    project, co, up, down = (
        Gather(at, buf, gather_send.at[i], gather_recv.at[i])
        for i, buf in enumerate((w_buf, co_buf.at[at.x], up_buf, down_buf))
    )
    kv = Lines(at, kv_buf, kv_send, kv_recv)
    ask = Direct(direct_send.at[2], direct_recv.at[2], at.z_peers())
    answer = Direct(direct_send.at[3], direct_recv.at[3], at.z_peers())
    answer_stat = Direct(direct_send.at[4], direct_recv.at[4], at.z_peers())
    co_x = Across(at, co_buf, across_send, across_recv)
    added, grad = (
        Scatter(at, *(ref.at[i] for ref in (part, from_x, total, from_w, x_send, x_recv, w_send, w_recv)))
        for i in range(2)
    )
    spread = Spread(at, spread_buf, spread_send, spread_recv)
    heads = Direct(direct_send.at[0], direct_recv.at[0], at.x_peers())
    feats = Direct(direct_send.at[1], direct_recv.at[1], at.w_peers())

    def own(gather):
        return gather.slot(at.z, at.y, at.c)

    loads = [
        pltpu.make_async_copy(src, dst, local_sem.at[i])
        for i, (src, dst) in enumerate(
            (
                (control_project.at[0], own(project).at[:, 0:128]),
                (control_project.at[1], own(project).at[:, 128:256]),
                (control_project.at[2], own(project).at[:, 256:384]),
                (control_in, own_in),
                (control_output, own(co)),
                (query_gain, own_gain.at[0]),
                (key_gain, own_gain.at[1]),
                (base_up, own(up)),
                (base_down, own(down)),
                (row_pair(base_hidden, at.tensor), own_base),
                (cotangent, own_cot),
            )
        )
    ]
    for load in loads:
        load.start()
    pl.semaphore_wait(barrier, len(partners))

    for load in loads[0:3]:
        load.wait()
    project.start()
    project.both_ways(0)
    loads[3].wait()
    normed_in[...] = norm_rows(own_in[...].astype(F32))[0].astype(BF16)
    project.middle(False)
    for load in loads[4:]:
        load.wait()
    co.start()
    up.start()
    down.start()
    project.relay()
    project.finish()
    co.middle()
    co_x.start(0)
    project.settle()
    projected = jnp.dot(normed_in[...], w_buf[...].reshape(D, 384), preferred_element_type=F32)
    kv_buf[at.y, at.c, :, 0:128] = head_norm(projected[:, 128:256], own_gain[1])
    kv_buf[at.y, at.c, :, 128:256] = projected[:, 256:384].astype(BF16)
    kv.start()
    q_buf[at.z] = head_norm(projected[:, 0:128], own_gain[0])
    for j in (2, 1, 3):
        ask.copy(j, q_buf.at[at.z], q_buf.at[at.z]).start()
    co.relay()
    co_x.start(-1, 1)
    kv.middle()
    co.finish()
    co_x.start(2)
    up.middle()
    for j in (1, 3, 2):
        ask.copy(j, q_buf.at[at.z], q_buf.at[at.zs(-j)]).wait_recv()
    kv.settle()
    asked = q_buf[...].reshape(512, 128)
    for y in range(4):
        block = kv_buf[y].reshape(256, 256)[:, 0:128]
        scores[y * 256 : (y + 1) * 256, :] = times_transposed(block, asked) * (1.0 / 128**0.5)
    values = kv_buf[...].reshape(1024, 256)[:, 128:256]
    for z in range(4):
        block = scores[:, z * 128 : (z + 1) * 128]
        top = jnp.max(block, axis=0, keepdims=True)
        expo = jnp.exp(block - top)
        sums = jnp.sum(expo, axis=0, keepdims=True)
        stat[z] = jnp.concatenate([top, sums, jnp.zeros((6, 128), F32)], axis=0)
        accum = lax.dot_general(
            values, expo.astype(BF16), (((0,), (0,)), ((), ())), preferred_element_type=F32
        )
        mix32[z] = accum
        mix16[z] = accum.astype(BF16)
    for j in (2, 1, 3):
        answer.copy(j, mix16.at[at.zs(j)], mix_back.at[j - 1]).start()
        answer_stat.copy(j, stat.at[at.zs(j)], stat_back.at[j - 1]).start()
    co.settle()
    co_x.swap()
    down.middle()
    accums, stats = [mix32[at.z]], [stat[at.z]]
    for j in (1, 3, 2):
        answer.copy(j, mix16.at[at.zs(j)], mix_back.at[j - 1]).wait_recv()
        answer_stat.copy(j, stat.at[at.zs(j)], stat_back.at[j - 1]).wait_recv()
        accums.append(mix_back[j - 1].astype(F32))
        stats.append(stat_back[j - 1])
    top = functools.reduce(jnp.maximum, [each[0:1] for each in stats])
    shares = [jnp.exp(each[0:1] - top) for each in stats]
    row_sum = sum(share * each[1:2] for share, each in zip(shares, stats))
    mixed = sum(share * each for share, each in zip(shares, accums)) / row_sum
    mixed = jnp.transpose(mixed).reshape(4, 4, 8, 128)
    for x in range(4):
        mix_send[x] = mixed[:, x].reshape(32, 128).astype(BF16)
    for j in (1, 3, 2):
        heads.copy(j, mix_send.at[at.xs(j)], mix_recv.at[at.x]).start()
    mix_recv[at.x] = mix_send[at.x]
    up.relay()
    co_x.settle()
    for j in (1, 3, 2):
        heads.copy(j, mix_send.at[at.xs(j)], mix_recv.at[at.xs(-j)]).wait_recv()
    mixed = jnp.concatenate([mix_recv[x] for x in range(4)], axis=1)
    for n in range(4):
        low, high = (
            times_transposed(
                mixed, jnp.concatenate([row_block(co_buf.at[x], m) for x in range(4)], axis=1)
            ).reshape(4, 8, 384)
            for m in (n, n + 4)
        )
        both = jnp.concatenate([low, high], axis=1)
        feat32[:, :, n * 384 : (n + 1) * 384] = both
        feat16[:, :, n * 384 : (n + 1) * 384] = both.astype(BF16)
    for j in (2, 1, 3):
        feats.copy(j, feat16.at[at.ws(j)], feat_recv.at[j - 1]).start()
    down.relay()
    up.finish()
    down.finish()
    feat = feat32[at.w]
    for j in (1, 3, 2):
        feats.copy(j, feat16.at[at.ws(j)], feat_recv.at[j - 1]).wait_recv()
        feat = feat + feat_recv[j - 1].astype(F32)
    summed = own_rows(own_base[...], at.tensor) + jnp.concatenate([feat[0:8], feat[8:16]], axis=1)
    nhat, rstd = norm_rows(summed)
    spread_buf[at.w, at.x] = jnp.concatenate([nhat[:, :HALF], nhat[:, HALF:]], axis=0).astype(BF16)
    spread.start()
    up.settle()
    down.settle()
    hidden_grad[...] = jnp.dot(
        own_cot[...], down_buf[...].reshape(D, 384), preferred_element_type=F32
    ).reshape(4, 32, 384)

    def mlp(*groups):
        for j in groups:
            spread.settle(j)
            w = at.ws(-j)
            blocks = [spread_buf[w, x].astype(F32) for x in range(4)]
            for k in (0, 2):
                for h in range(2):
                    normed[j, k * 8 : k * 8 + 16, h * HALF : (h + 1) * HALF] = jnp.concatenate(
                        [block[h * 8 : (h + 1) * 8] for block in blocks[k : k + 2]], axis=0
                    ).astype(BF16)
        pre = jnp.dot(
            jnp.concatenate([normed[j] for j in groups], axis=0), up_buf[...].reshape(D, 384), preferred_element_type=F32
        )
        tangent = jnp.tanh(0.7978845608028654 * (pre + 0.044715 * pre * pre * pre))
        hidden = (0.5 * pre * (1.0 + tangent)).astype(BF16)
        slope = 0.5 * (1.0 + tangent) + 0.5 * pre * (1.0 - tangent * tangent) * 0.7978845608028654 * (
            1.0 + 3.0 * 0.044715 * pre * pre
        )
        arriving = jnp.concatenate([hidden_grad[at.ws(-j)] for j in groups], axis=0)
        added.fill(groups, hidden, down_buf)
        grad.fill(groups, (arriving * slope).astype(BF16), up_buf)

    mlp(0)
    spread.forward(1)
    spread.forward(3)
    spread.forward(2)
    mlp(1, 3)
    mlp(2)
    for j in (1, 3, 2):
        added.pass_on(j)
        grad.pass_on(j)
    base_out[...] = summed + added.done()
    normed_grad = grad.done()
    feat_grad[...] = own_rows(row_pair(own_cot, at.tensor)[...], at.tensor) + rstd * (
        normed_grad
        - jnp.mean(normed_grad, axis=-1, keepdims=True)
        - nhat * jnp.mean(normed_grad * nhat, axis=-1, keepdims=True)
    )
    for each in (project, kv, co, up, down, co_x, spread, added, grad):
        each.drain()
    for j in (1, 2, 3):
        ask.copy(j, q_buf.at[at.z], q_buf.at[at.z]).wait_send()
        answer.copy(j, mix16.at[at.zs(j)], mix_back.at[j - 1]).wait_send()
        answer_stat.copy(j, stat.at[at.zs(j)], stat_back.at[j - 1]).wait_send()
        heads.copy(j, mix_send.at[at.xs(j)], mix_recv.at[at.x]).wait_send()
        feats.copy(j, feat16.at[at.ws(j)], feat_recv.at[j - 1]).wait_send()


def body(*args):
    args = list(args)
    args[3] = args[3].reshape(1, 128)
    args[4] = args[4].reshape(1, 128)
    vmem = pl.BlockSpec(memory_space=pltpu.VMEM)
    out = pl.pallas_call(
        kernel,
        out_shape=[jax.ShapeDtypeStruct((8, D), F32)] * 2,
        in_specs=[pl.BlockSpec(memory_space=pltpu.HBM)] * 9,
        out_specs=[vmem] * 2,
        scratch_shapes=[
            pltpu.VMEM((4, 4, 2, 96, 384), BF16),
            pltpu.VMEM((4, 2, 128, 256), BF16),
            pltpu.VMEM((4, 128, 128), BF16),
            pltpu.VMEM((4, 4, 4, 2, 96, 128), BF16),
            pltpu.VMEM((4, 4, 2, 96, 384), BF16),
            pltpu.VMEM((4, 4, 2, 96, 384), BF16),
            pltpu.VMEM((128, D), BF16),
            pltpu.VMEM((2, 1, 128), F32),
            pltpu.VMEM((16, D), BF16),
            pltpu.VMEM((128, D), BF16),
            pltpu.VMEM((128, D), BF16),
            pltpu.VMEM((1024, 512), F32),
            pltpu.VMEM((4, 8, 128), F32),
            pltpu.VMEM((3, 8, 128), F32),
            pltpu.VMEM((4, 128, 128), F32),
            pltpu.VMEM((4, 128, 128), BF16),
            pltpu.VMEM((3, 128, 128), BF16),
            pltpu.VMEM((4, 32, 128), BF16),
            pltpu.VMEM((4, 32, 128), BF16),
            pltpu.VMEM((4, 16, HALF), F32),
            pltpu.VMEM((4, 16, HALF), BF16),
            pltpu.VMEM((3, 16, HALF), BF16),
            pltpu.VMEM((4, 4, 16, HALF), BF16),
            pltpu.VMEM((4, 32, D), BF16),
            pltpu.VMEM((4, 32, 384), F32),
            pltpu.VMEM((2, 4, 4, 16, HALF), BF16),
            pltpu.VMEM((2, 4, 3, 16, HALF), BF16),
            pltpu.VMEM((2, 3, 16, HALF), BF16),
            pltpu.VMEM((2, 3, 16, HALF), BF16),
            pltpu.SemaphoreType.DMA((11,)),
            pltpu.SemaphoreType.DMA((4, 4)),
            pltpu.SemaphoreType.DMA((4, 19)),
            pltpu.SemaphoreType.DMA((7,)),
            pltpu.SemaphoreType.DMA((7,)),
            pltpu.SemaphoreType.DMA((2,)),
            pltpu.SemaphoreType.DMA((15,)),
            pltpu.SemaphoreType.DMA((5, 3)),
            pltpu.SemaphoreType.DMA((5, 3)),
            pltpu.SemaphoreType.DMA((2,)),
            pltpu.SemaphoreType.DMA((2, 12)),
            pltpu.SemaphoreType.DMA((2,)),
            pltpu.SemaphoreType.DMA((2, 3)),
            pltpu.SemaphoreType.DMA((2,)),
            pltpu.SemaphoreType.DMA((15,)),
        ],
        compiler_params=pltpu.CompilerParams(
            collective_id=0, has_side_effects=True, vmem_limit_bytes=64000 * 1024
        ),
    )(*args)
    return tuple(each.astype(BF16) for each in out)


def solution(mesh):
    placed = (
        P("dp", None),
        P(None, "dp", "tensor"),
        P("dp", "tensor"),
        P(),
        P(),
        P("dp", None),
        P("dp", "tensor"),
        P("dp", "tensor"),
        P("dp", None),
    )
    return jax.shard_map(
        body,
        mesh=mesh,
        in_specs=placed,
        out_specs=(P(("dp", "tensor"), None), P(("dp", "tensor"), None)),
        check_vma=False,
    )
```

```python
import functools

import jax
import jax.numpy as jnp
from jax import lax
from jax.experimental import pallas as pl
from jax.experimental.pallas import tpu as pltpu
from jax.sharding import PartitionSpec as P

F32 = jnp.float32
BF16 = jnp.bfloat16
MESH = pl.DeviceIdType.MESH
D = 3072
HALF = D // 2


def norm_rows(values):
    center = values - jnp.mean(values, axis=-1, keepdims=True)
    spread = jnp.mean(center * center, axis=-1, keepdims=True)
    rstd = lax.rsqrt(spread + 1e-06)
    return (center * rstd, rstd)


def head_norm(values, gain):
    square_mean = jnp.mean(values * values, axis=-1, keepdims=True)
    return (values * lax.rsqrt(square_mean + 1e-06) * gain).astype(BF16)


def times_transposed(left, right):
    return lax.dot_general(left, right, (((1,), (1,)), ((), ())), preferred_element_type=F32)


class Place:
    def __init__(self):
        dp, tensor = lax.axis_index("dp"), lax.axis_index("tensor")
        self.dp, self.tensor = dp, tensor
        self.z, self.y, self.c = dp // 8, lax.rem(dp // 2, 4), lax.rem(dp, 2)
        self.w, self.x = tensor // 4, lax.rem(tensor, 4)
        self.sibling = self.at(self.z, self.y, 1 - self.c)

    def at(self, z, y, c):
        return (z * 8 + y * 2 + c, self.tensor)

    def zs(self, j):
        return lax.rem(self.z + (j + 4), 4)

    def ys(self, j):
        return lax.rem(self.y + (j + 4), 4)

    def xs(self, j):
        return lax.rem(self.x + (j + 4), 4)

    def ws(self, j):
        return lax.rem(self.w + (j + 4), 4)

    def tensor_at(self, w, x):
        return (self.dp, w * 4 + x)

    def partners(self):
        return (
            self.z_peers()
            + self.y_peers()
            + [self.sibling]
            + self.x_peers()
            + self.w_peers()
        )

    def z_peers(self):
        return [self.at(self.zs(j), self.y, self.c) for j in (1, 2, 3)]

    def y_peers(self):
        return [self.at(self.z, self.ys(j), self.c) for j in (1, 2, 3)]

    def x_peers(self):
        return [self.tensor_at(self.w, self.xs(j)) for j in (1, 2, 3)]

    def w_peers(self):
        return [self.tensor_at(self.ws(j), self.x) for j in (1, 2, 3)]


def remote(src, dst, send, recv, device):
    return pltpu.make_async_remote_copy(
        src_ref=src, dst_ref=dst, send_sem=send, recv_sem=recv, device_id=device, device_id_type=MESH
    )


class Gather:
    def __init__(self, at, buf, send, recv):
        self.at, self.buf, self.send, self.recv = at, buf, send, recv

    def slot(self, z, y, c):
        return self.buf.at[z, y, c]

    def line(self, y, c):
        return self.buf.at[:, y, c]

    def copy(self, ref, group, sem, device):
        return remote(ref, ref, self.send.at[group], self.recv.at[sem], device)

    def wait(self, ref, sem):
        self.copy(ref, 0, sem, self.at.sibling).wait_recv()

    def both_ways(self, j):
        at = self.at
        ref = self.slot(at.zs(-j), at.y, at.c)
        self.copy(ref, 1, 3 + j, at.at(at.z, at.ys(1), at.c)).start()
        self.copy(ref, 1, 7 + j, at.at(at.z, at.ys(-1), at.c)).start()

    def start(self):
        at = self.at
        for j in (1, 3, 2):
            self.copy(self.slot(at.z, at.y, at.c), 0, j - 1, at.at(at.zs(j), at.y, at.c)).start()

    def middle(self, own=True):
        at = self.at
        if own:
            self.both_ways(0)
        for j in (1, 3, 2):
            self.wait(self.slot(at.zs(-j), at.y, at.c), j - 1)
            self.both_ways(j)
        self.copy(self.line(at.y, at.c), 3, 15, at.sibling).start()

    def relay(self):
        at = self.at
        for j in (0, 1, 3, 2):
            below, above = self.slot(at.zs(-j), at.ys(-1), at.c), self.slot(at.zs(-j), at.ys(1), at.c)
            self.wait(below, 3 + j)
            if j in (0, 3):
                self.copy(below, 2, 11 + j, at.at(at.z, at.ys(1), at.c)).start()
            self.wait(above, 7 + j)
            if j in (1, 2):
                self.copy(above, 2, 11 + j, at.at(at.z, at.ys(-1), at.c)).start()
        self.copy(self.line(at.ys(-1), at.c), 3, 16, at.sibling).start()
        self.copy(self.line(at.ys(1), at.c), 3, 17, at.sibling).start()

    def finish(self):
        at = self.at
        for j in (0, 1, 3, 2):
            self.wait(self.slot(at.zs(-j), at.ys(2), at.c), 11 + j)
        self.copy(self.line(at.ys(2), at.c), 3, 18, at.sibling).start()

    def settle(self):
        at = self.at
        for sem, step in ((15, 0), (16, -1), (17, 1), (18, 2)):
            self.wait(self.line(at.ys(step), 1 - at.c), sem)

    def drain(self):
        buf = self.buf
        for group, ref in enumerate((buf.at[0:3, 0, 0], buf.at[:, 0], buf.at[:, 0, 0], buf.at[:, :, 0])):
            self.copy(ref, group, 0, self.at.sibling).wait_send()


class Across:
    def __init__(self, at, buf, send, recv):
        self.at, self.buf, self.send, self.recv = at, buf, send, recv

    def line(self, x, step):
        return self.buf.at[x, :, self.at.ys(step), self.at.c]

    def copy(self, ref, group, sem, device):
        return remote(ref, ref, self.send.at[group], self.recv.at[sem], device)

    def start(self, *steps):
        at = self.at
        for step in steps:
            for i in (1, 3, 2):
                self.copy(self.line(at.x, step), 0, (step + 1) * 3 + i - 1, at.tensor_at(at.w, at.xs(i))).start()

    def swap(self):
        at = self.at
        for i in (1, 3, 2):
            for step in (0, -1, 1, 2):
                self.copy(self.line(at.xs(-i), step), 0, (step + 1) * 3 + i - 1, at.sibling).wait_recv()
            self.copy(self.buf.at[at.xs(-i), :, :, at.c], 1, 12 + i - 1, at.sibling).start()

    def settle(self):
        at = self.at
        for i in (1, 3, 2):
            self.copy(self.buf.at[at.xs(-i), :, :, 1 - at.c], 1, 12 + i - 1, at.sibling).wait_recv()

    def drain(self):
        for group in range(2):
            self.copy(self.buf.at[0:3, :, :, 0], group, 0, self.at.sibling).wait_send()


class Scatter:
    def __init__(self, at, part, from_x, total, from_w, x_send, x_recv, w_send, w_recv):
        self.at, self.part, self.from_x, self.total, self.from_w = at, part, from_x, total, from_w
        self.x_send, self.x_recv, self.w_send, self.w_recv = x_send, x_recv, w_send, w_recv

    def x_copy(self, j, i):
        at = self.at
        return remote(
            self.part.at[j, at.xs(i)], self.from_x.at[j, i - 1], self.x_send, self.x_recv.at[3 * j + i - 1],
            at.tensor_at(at.w, at.xs(i)),
        )

    def w_copy(self, j):
        at = self.at
        return remote(
            self.total.at[j - 1], self.from_w.at[j - 1], self.w_send, self.w_recv.at[j - 1],
            at.tensor_at(at.ws(-j), at.x),
        )

    def half_copy(self, h):
        at, lanes = self.at, pl.ds(h * (HALF // 2), HALF // 2)
        return remote(
            self.total.at[1, :, lanes], self.from_w.at[1, :, lanes], self.w_send, self.w_recv.at[3 if h else 1],
            at.tensor_at(at.ws(-1 if h else 1), at.x),
        )

    def fill(self, groups, left, matrix):
        for n in range(4):
            low, high = (
                times_transposed(left, row_block(matrix, m)).reshape(4 * len(groups), 8, 384) for m in (n, n + 4)
            )
            both = jnp.concatenate([low, high], axis=1).astype(BF16)
            for k, j in enumerate(groups):
                for x in range(4):
                    self.part[j, x, :, n * 384 : (n + 1) * 384] = both[4 * k + x]
        for j in groups:
            for i in (1, 3, 2):
                self.x_copy(j, i).start()

    def sum_x(self, j):
        total = self.part[j, self.at.x].astype(F32)
        for i in (1, 3, 2):
            self.x_copy(j, i).wait_recv()
            total = total + self.from_x[j, i - 1].astype(F32)
        return total

    def far(self):
        self.total[1] = self.sum_x(2).astype(BF16)
        for h in range(2):
            self.half_copy(h).start()

    def near(self, j):
        h = 1 if j == 1 else 0
        total = self.sum_x(j)
        self.half_copy(h).wait_recv()
        low, high = total[:, : HALF // 2], total[:, HALF // 2 :]
        half = self.from_w[1, :, h * (HALF // 2) : (h + 1) * (HALF // 2)].astype(F32)
        total = jnp.concatenate([low, high + half] if h else [low + half, high], axis=1)
        self.total[j - 1] = total.astype(BF16)
        self.w_copy(j).start()

    def done(self):
        total = self.sum_x(0)
        for j in (1, 3):
            self.w_copy(j).wait_recv()
            total = total + self.from_w[j - 1].astype(F32)
        return jnp.concatenate([total[0:8], total[8:16]], axis=1)

    def drain(self):
        at = self.at
        whole = self.part.at[0:3]
        remote(whole, whole, self.x_send, self.x_recv.at[0], at.sibling).wait_send()
        remote(self.total, self.total, self.w_send, self.w_recv.at[0], at.sibling).wait_send()


class Direct:
    def __init__(self, send, recv, peers):
        self.send, self.recv, self.peers = send, recv, peers

    def copy(self, j, src, dst):
        return remote(src, dst, self.send.at[j - 1], self.recv.at[j - 1], self.peers[j - 1])


class Lines:
    def __init__(self, at, buf, send, recv):
        self.at, self.buf, self.send, self.recv = at, buf, send, recv

    def copy(self, i, other=False):
        at = self.at
        ref = self.buf.at[at.ys(-i), 1 - at.c if other else at.c]
        return remote(ref, ref, self.send.at[3 + i], self.recv.at[3 + i], at.sibling)

    def along_y(self, i):
        at = self.at
        ref = self.buf.at[at.y, at.c]
        return remote(ref, ref, self.send.at[i - 1], self.recv.at[i - 1], at.y_peers()[i - 1])

    def start(self):
        for i in (2, 1, 3):
            self.along_y(i).start()
        self.copy(0).start()

    def middle(self):
        at = self.at
        for i in (1, 3, 2):
            ref = self.buf.at[at.ys(-i), at.c]
            remote(ref, ref, self.send.at[i - 1], self.recv.at[i - 1], at.sibling).wait_recv()
            self.copy(i).start()

    def settle(self):
        for i in (0, 1, 3, 2):
            self.copy(i, True).wait_recv()

    def drain(self):
        for i in (1, 2, 3):
            self.along_y(i).wait_send()
        for i in range(4):
            self.copy(i).wait_send()


class Spread:
    def __init__(self, at, buf, send, recv):
        self.at, self.buf, self.send, self.recv = at, buf, send, recv

    def copy(self, ref, group, sem, device):
        return remote(ref, ref, self.send.at[group], self.recv.at[sem], device)

    def along_x(self, j):
        at = self.at
        for i in (1, 3, 2):
            self.copy(self.buf.at[at.ws(-j), at.x], 1, 3 + 3 * j + i - 1, at.tensor_at(at.w, at.xs(i))).start()

    def start(self):
        at = self.at
        for j in (1, 3):
            self.copy(self.buf.at[at.w, at.x], 0, j - 1, at.tensor_at(at.ws(j), at.x)).start()
        self.along_x(0)

    def half(self, j, h):
        return self.buf.at[self.at.ws(-j), self.at.x, :, pl.ds(h * (HALF // 2), HALF // 2)]

    def forward(self, j):
        at = self.at
        if j == 2:
            self.copy(self.half(2, 0), 0, 1, at.sibling).wait_recv()
            self.copy(self.half(2, 1), 0, 15, at.sibling).wait_recv()
        else:
            self.copy(self.buf.at[at.ws(-j), at.x], 0, j - 1, at.sibling).wait_recv()
            h = 0 if j == 1 else 1
            self.copy(self.half(j, h), 0, 15 if h else 1, at.tensor_at(at.ws(j), at.x)).start()
        self.along_x(j)

    def settle(self, j):
        at = self.at
        for i in (1, 3, 2):
            self.copy(self.buf.at[at.ws(-j), at.xs(-i)], 1, 3 + 3 * j + i - 1, at.sibling).wait_recv()

    def drain(self):
        self.copy(self.buf.at[0:3, 0], 0, 0, self.at.sibling).wait_send()
        self.copy(self.buf.at[0:3], 1, 0, self.at.sibling).wait_send()


def row_block(matrix, n):
    y = 2 * (n % 2)
    return matrix[n // 2, y : y + 2].reshape(384, matrix.shape[-1])


def row_pair(ref, tensor):
    return ref.at[pl.ds(pl.multiple_of((tensor // 2) * 16, 16), 16), :]


def own_rows(pair, tensor):
    pair = pair.astype(F32)
    return jnp.where(lax.rem(tensor, 2) == 0, pair[0:8], pair[8:16])


def kernel(
    control_in, control_project, control_output, query_gain, key_gain, base_hidden, base_up, base_down, cotangent,
    base_out, feat_grad,
    w_buf, kv_buf, q_buf, co_buf, up_buf, down_buf, own_in, own_gain, own_base, own_cot,
    normed_in, scores, stat, stat_back, mix32, mix16, mix_back, mix_send, mix_recv, feat32, feat16, feat_recv, spread_buf, normed, hidden_grad,
    part, from_x, total, from_w,
    local_sem, gather_send, gather_recv, kv_send, kv_recv, across_send, across_recv, direct_send, direct_recv,
    x_send, x_recv, w_send, w_recv, spread_send, spread_recv,
):
    at = Place()
    barrier = pltpu.get_barrier_semaphore()
    partners = at.partners()
    for device in partners:
        pl.semaphore_signal(barrier, inc=1, device_id=device, device_id_type=MESH)

    project, co, up, down = (
        Gather(at, buf, gather_send.at[i], gather_recv.at[i])
        for i, buf in enumerate((w_buf, co_buf.at[at.x], up_buf, down_buf))
    )
    kv = Lines(at, kv_buf, kv_send, kv_recv)
    ask = Direct(direct_send.at[2], direct_recv.at[2], at.z_peers())
    answer = Direct(direct_send.at[3], direct_recv.at[3], at.z_peers())
    answer_stat = Direct(direct_send.at[4], direct_recv.at[4], at.z_peers())
    co_x = Across(at, co_buf, across_send, across_recv)
    added, grad = (
        Scatter(at, *(ref.at[i] for ref in (part, from_x, total, from_w, x_send, x_recv, w_send, w_recv)))
        for i in range(2)
    )
    spread = Spread(at, spread_buf, spread_send, spread_recv)
    heads = Direct(direct_send.at[0], direct_recv.at[0], at.x_peers())
    feats = Direct(direct_send.at[1], direct_recv.at[1], at.w_peers())

    def own(gather):
        return gather.slot(at.z, at.y, at.c)

    loads = [
        pltpu.make_async_copy(src, dst, local_sem.at[i])
        for i, (src, dst) in enumerate(
            (
                (control_project.at[0], own(project).at[:, 0:128]),
                (control_project.at[1], own(project).at[:, 128:256]),
                (control_project.at[2], own(project).at[:, 256:384]),
                (control_in, own_in),
                (control_output, own(co)),
                (query_gain, own_gain.at[0]),
                (key_gain, own_gain.at[1]),
                (base_up, own(up)),
                (base_down, own(down)),
                (row_pair(base_hidden, at.tensor), own_base),
                (cotangent, own_cot),
            )
        )
    ]
    for load in loads:
        load.start()
    pl.semaphore_wait(barrier, len(partners))

    for load in loads[0:3]:
        load.wait()
    project.start()
    project.both_ways(0)
    loads[3].wait()
    normed_in[...] = norm_rows(own_in[...].astype(F32))[0].astype(BF16)
    project.middle(False)
    for load in loads[4:]:
        load.wait()
    co.start()
    project.relay()
    co.middle()
    co_x.start(0)
    up.start()
    down.start()
    project.finish()
    co.relay()
    co_x.start(-1, 1)
    project.settle()
    projected = jnp.dot(normed_in[...], w_buf[...].reshape(D, 384), preferred_element_type=F32)
    kv_buf[at.y, at.c, :, 0:128] = head_norm(projected[:, 128:256], own_gain[1])
    kv_buf[at.y, at.c, :, 128:256] = projected[:, 256:384].astype(BF16)
    kv.start()
    q_buf[at.z] = head_norm(projected[:, 0:128], own_gain[0])
    for j in (2, 1, 3):
        ask.copy(j, q_buf.at[at.z], q_buf.at[at.z]).start()
    kv.middle()
    co.finish()
    co_x.start(2)
    up.middle()
    for j in (1, 3, 2):
        ask.copy(j, q_buf.at[at.z], q_buf.at[at.zs(-j)]).wait_recv()
    kv.settle()
    asked = q_buf[...].reshape(512, 128)
    for y in range(4):
        block = kv_buf[y].reshape(256, 256)[:, 0:128]
        scores[y * 256 : (y + 1) * 256, :] = times_transposed(block, asked) * (1.0 / 128**0.5)
    values = kv_buf[...].reshape(1024, 256)[:, 128:256]
    for z in range(4):
        block = scores[:, z * 128 : (z + 1) * 128]
        top = jnp.max(block, axis=0, keepdims=True)
        expo = jnp.exp(block - top)
        sums = jnp.sum(expo, axis=0, keepdims=True)
        stat[z] = jnp.concatenate([top, sums, jnp.zeros((6, 128), F32)], axis=0)
        accum = lax.dot_general(
            values, expo.astype(BF16), (((0,), (0,)), ((), ())), preferred_element_type=F32
        )
        mix32[z] = accum
        mix16[z] = accum.astype(BF16)
    for j in (2, 1, 3):
        answer.copy(j, mix16.at[at.zs(j)], mix_back.at[j - 1]).start()
        answer_stat.copy(j, stat.at[at.zs(j)], stat_back.at[j - 1]).start()
    co.settle()
    co_x.swap()
    down.middle()
    accums, stats = [mix32[at.z]], [stat[at.z]]
    for j in (1, 3, 2):
        answer.copy(j, mix16.at[at.zs(j)], mix_back.at[j - 1]).wait_recv()
        answer_stat.copy(j, stat.at[at.zs(j)], stat_back.at[j - 1]).wait_recv()
        accums.append(mix_back[j - 1].astype(F32))
        stats.append(stat_back[j - 1])
    top = functools.reduce(jnp.maximum, [each[0:1] for each in stats])
    shares = [jnp.exp(each[0:1] - top) for each in stats]
    row_sum = sum(share * each[1:2] for share, each in zip(shares, stats))
    mixed = sum(share * each for share, each in zip(shares, accums)) / row_sum
    mixed = jnp.transpose(mixed).reshape(4, 4, 8, 128)
    for x in range(4):
        mix_send[x] = mixed[:, x].reshape(32, 128).astype(BF16)
    for j in (1, 3, 2):
        heads.copy(j, mix_send.at[at.xs(j)], mix_recv.at[at.x]).start()
    mix_recv[at.x] = mix_send[at.x]
    up.relay()
    co_x.settle()
    for j in (1, 3, 2):
        heads.copy(j, mix_send.at[at.xs(j)], mix_recv.at[at.xs(-j)]).wait_recv()
    mixed = jnp.concatenate([mix_recv[x] for x in range(4)], axis=1)
    for n in range(4):
        low, high = (
            times_transposed(
                mixed, jnp.concatenate([row_block(co_buf.at[x], m) for x in range(4)], axis=1)
            ).reshape(4, 8, 384)
            for m in (n, n + 4)
        )
        both = jnp.concatenate([low, high], axis=1)
        feat32[:, :, n * 384 : (n + 1) * 384] = both
        feat16[:, :, n * 384 : (n + 1) * 384] = both.astype(BF16)
    for j in (2, 1, 3):
        feats.copy(j, feat16.at[at.ws(j)], feat_recv.at[j - 1]).start()
    down.relay()
    up.finish()
    down.finish()
    feat = feat32[at.w]
    for j in (1, 3, 2):
        feats.copy(j, feat16.at[at.ws(j)], feat_recv.at[j - 1]).wait_recv()
        feat = feat + feat_recv[j - 1].astype(F32)
    summed = own_rows(own_base[...], at.tensor) + jnp.concatenate([feat[0:8], feat[8:16]], axis=1)
    nhat, rstd = norm_rows(summed)
    spread_buf[at.w, at.x] = jnp.concatenate([nhat[:, :HALF], nhat[:, HALF:]], axis=0).astype(BF16)
    spread.start()
    up.settle()
    down.settle()
    hidden_grad[...] = jnp.dot(
        own_cot[...], down_buf[...].reshape(D, 384), preferred_element_type=F32
    ).reshape(4, 32, 384)

    def mlp(*groups):
        for j in groups:
            spread.settle(j)
            w = at.ws(-j)
            blocks = [spread_buf[w, x].astype(F32) for x in range(4)]
            for k in (0, 2):
                for h in range(2):
                    normed[j, k * 8 : k * 8 + 16, h * HALF : (h + 1) * HALF] = jnp.concatenate(
                        [block[h * 8 : (h + 1) * 8] for block in blocks[k : k + 2]], axis=0
                    ).astype(BF16)
        pre = jnp.dot(
            jnp.concatenate([normed[j] for j in groups], axis=0), up_buf[...].reshape(D, 384), preferred_element_type=F32
        )
        tangent = jnp.tanh(0.7978845608028654 * (pre + 0.044715 * pre * pre * pre))
        hidden = (0.5 * pre * (1.0 + tangent)).astype(BF16)
        slope = 0.5 * (1.0 + tangent) + 0.5 * pre * (1.0 - tangent * tangent) * 0.7978845608028654 * (
            1.0 + 3.0 * 0.044715 * pre * pre
        )
        arriving = jnp.concatenate([hidden_grad[at.ws(-j)] for j in groups], axis=0)
        added.fill(groups, hidden, down_buf)
        grad.fill(groups, (arriving * slope).astype(BF16), up_buf)

    mlp(0)
    spread.forward(1)
    spread.forward(3)
    spread.forward(2)
    mlp(2, 1, 3)
    added.far()
    grad.far()
    for j in (1, 3):
        added.near(j)
    for j in (1, 3):
        grad.near(j)
    base_out[...] = summed + added.done()
    normed_grad = grad.done()
    feat_grad[...] = own_rows(row_pair(own_cot, at.tensor)[...], at.tensor) + rstd * (
        normed_grad
        - jnp.mean(normed_grad, axis=-1, keepdims=True)
        - nhat * jnp.mean(normed_grad * nhat, axis=-1, keepdims=True)
    )
    for each in (project, kv, co, up, down, co_x, spread, added, grad):
        each.drain()
    for j in (1, 2, 3):
        ask.copy(j, q_buf.at[at.z], q_buf.at[at.z]).wait_send()
        answer.copy(j, mix16.at[at.zs(j)], mix_back.at[j - 1]).wait_send()
        answer_stat.copy(j, stat.at[at.zs(j)], stat_back.at[j - 1]).wait_send()
        heads.copy(j, mix_send.at[at.xs(j)], mix_recv.at[at.x]).wait_send()
        feats.copy(j, feat16.at[at.ws(j)], feat_recv.at[j - 1]).wait_send()


def body(*args):
    args = list(args)
    args[3] = args[3].reshape(1, 128)
    args[4] = args[4].reshape(1, 128)
    vmem = pl.BlockSpec(memory_space=pltpu.VMEM)
    out = pl.pallas_call(
        kernel,
        out_shape=[jax.ShapeDtypeStruct((8, D), F32)] * 2,
        in_specs=[pl.BlockSpec(memory_space=pltpu.HBM)] * 9,
        out_specs=[vmem] * 2,
        scratch_shapes=[
            pltpu.VMEM((4, 4, 2, 96, 384), BF16),
            pltpu.VMEM((4, 2, 128, 256), BF16),
            pltpu.VMEM((4, 128, 128), BF16),
            pltpu.VMEM((4, 4, 4, 2, 96, 128), BF16),
            pltpu.VMEM((4, 4, 2, 96, 384), BF16),
            pltpu.VMEM((4, 4, 2, 96, 384), BF16),
            pltpu.VMEM((128, D), BF16),
            pltpu.VMEM((2, 1, 128), F32),
            pltpu.VMEM((16, D), BF16),
            pltpu.VMEM((128, D), BF16),
            pltpu.VMEM((128, D), BF16),
            pltpu.VMEM((1024, 512), F32),
            pltpu.VMEM((4, 8, 128), F32),
            pltpu.VMEM((3, 8, 128), F32),
            pltpu.VMEM((4, 128, 128), F32),
            pltpu.VMEM((4, 128, 128), BF16),
            pltpu.VMEM((3, 128, 128), BF16),
            pltpu.VMEM((4, 32, 128), BF16),
            pltpu.VMEM((4, 32, 128), BF16),
            pltpu.VMEM((4, 16, HALF), F32),
            pltpu.VMEM((4, 16, HALF), BF16),
            pltpu.VMEM((3, 16, HALF), BF16),
            pltpu.VMEM((4, 4, 16, HALF), BF16),
            pltpu.VMEM((4, 32, D), BF16),
            pltpu.VMEM((4, 32, 384), F32),
            pltpu.VMEM((2, 4, 4, 16, HALF), BF16),
            pltpu.VMEM((2, 4, 3, 16, HALF), BF16),
            pltpu.VMEM((2, 3, 16, HALF), BF16),
            pltpu.VMEM((2, 3, 16, HALF), BF16),
            pltpu.SemaphoreType.DMA((11,)),
            pltpu.SemaphoreType.DMA((4, 4)),
            pltpu.SemaphoreType.DMA((4, 19)),
            pltpu.SemaphoreType.DMA((7,)),
            pltpu.SemaphoreType.DMA((7,)),
            pltpu.SemaphoreType.DMA((2,)),
            pltpu.SemaphoreType.DMA((15,)),
            pltpu.SemaphoreType.DMA((5, 3)),
            pltpu.SemaphoreType.DMA((5, 3)),
            pltpu.SemaphoreType.DMA((2,)),
            pltpu.SemaphoreType.DMA((2, 12)),
            pltpu.SemaphoreType.DMA((2,)),
            pltpu.SemaphoreType.DMA((2, 4)),
            pltpu.SemaphoreType.DMA((2,)),
            pltpu.SemaphoreType.DMA((16,)),
        ],
        compiler_params=pltpu.CompilerParams(
            collective_id=0, has_side_effects=True, vmem_limit_bytes=64000 * 1024
        ),
    )(*args)
    return tuple(each.astype(BF16) for each in out)


def solution(mesh):
    placed = (
        P("dp", None),
        P(None, "dp", "tensor"),
        P("dp", "tensor"),
        P(),
        P(),
        P("dp", None),
        P("dp", "tensor"),
        P("dp", "tensor"),
        P("dp", None),
    )
    return jax.shard_map(
        body,
        mesh=mesh,
        in_specs=placed,
        out_specs=(P(("dp", "tensor"), None), P(("dp", "tensor"), None)),
        check_vma=False,
    )
```

```python
import functools

import jax
import jax.numpy as jnp
from jax import lax
from jax.experimental import pallas as pl
from jax.experimental.pallas import tpu as pltpu
from jax.sharding import PartitionSpec as P

F32 = jnp.float32
BF16 = jnp.bfloat16
MESH = pl.DeviceIdType.MESH
D = 3072
HALF = D // 2


def norm_rows(values):
    center = values - jnp.mean(values, axis=-1, keepdims=True)
    spread = jnp.mean(center * center, axis=-1, keepdims=True)
    rstd = lax.rsqrt(spread + 1e-06)
    return (center * rstd, rstd)


def head_norm(values, gain):
    square_mean = jnp.mean(values * values, axis=-1, keepdims=True)
    return (values * lax.rsqrt(square_mean + 1e-06) * gain).astype(BF16)


def times_transposed(left, right):
    return lax.dot_general(left, right, (((1,), (1,)), ((), ())), preferred_element_type=F32)


class Place:
    def __init__(self):
        dp, tensor = lax.axis_index("dp"), lax.axis_index("tensor")
        self.dp, self.tensor = dp, tensor
        self.z, self.y, self.c = dp // 8, lax.rem(dp // 2, 4), lax.rem(dp, 2)
        self.w, self.x = tensor // 4, lax.rem(tensor, 4)
        self.sibling = self.at(self.z, self.y, 1 - self.c)

    def at(self, z, y, c):
        return (z * 8 + y * 2 + c, self.tensor)

    def zs(self, j):
        return lax.rem(self.z + (j + 4), 4)

    def ys(self, j):
        return lax.rem(self.y + (j + 4), 4)

    def xs(self, j):
        return lax.rem(self.x + (j + 4), 4)

    def ws(self, j):
        return lax.rem(self.w + (j + 4), 4)

    def tensor_at(self, w, x):
        return (self.dp, w * 4 + x)

    def partners(self):
        return (
            self.z_peers()
            + self.y_peers()
            + [self.sibling]
            + self.x_peers()
            + self.w_peers()
        )

    def z_peers(self):
        return [self.at(self.zs(j), self.y, self.c) for j in (1, 2, 3)]

    def y_peers(self):
        return [self.at(self.z, self.ys(j), self.c) for j in (1, 2, 3)]

    def x_peers(self):
        return [self.tensor_at(self.w, self.xs(j)) for j in (1, 2, 3)]

    def w_peers(self):
        return [self.tensor_at(self.ws(j), self.x) for j in (1, 2, 3)]


def remote(src, dst, send, recv, device):
    return pltpu.make_async_remote_copy(
        src_ref=src, dst_ref=dst, send_sem=send, recv_sem=recv, device_id=device, device_id_type=MESH
    )


class Gather:
    def __init__(self, at, buf, send, recv):
        self.at, self.buf, self.send, self.recv = at, buf, send, recv

    def slot(self, z, y, c):
        return self.buf.at[z, y, c]

    def line(self, y, c):
        return self.buf.at[:, y, c]

    def copy(self, ref, group, sem, device):
        return remote(ref, ref, self.send.at[group], self.recv.at[sem], device)

    def wait(self, ref, sem):
        self.copy(ref, 0, sem, self.at.sibling).wait_recv()

    def both_ways(self, j):
        at = self.at
        ref = self.slot(at.zs(-j), at.y, at.c)
        self.copy(ref, 1, 3 + j, at.at(at.z, at.ys(1), at.c)).start()
        self.copy(ref, 1, 7 + j, at.at(at.z, at.ys(-1), at.c)).start()

    def start(self):
        at = self.at
        for j in (1, 3, 2):
            self.copy(self.slot(at.z, at.y, at.c), 0, j - 1, at.at(at.zs(j), at.y, at.c)).start()

    def middle(self, own=True):
        at = self.at
        if own:
            self.both_ways(0)
        for j in (1, 3, 2):
            self.wait(self.slot(at.zs(-j), at.y, at.c), j - 1)
            self.both_ways(j)
        self.copy(self.line(at.y, at.c), 3, 15, at.sibling).start()

    def relay(self):
        at = self.at
        for j in (0, 1, 3, 2):
            below, above = self.slot(at.zs(-j), at.ys(-1), at.c), self.slot(at.zs(-j), at.ys(1), at.c)
            self.wait(below, 3 + j)
            if j in (0, 3):
                self.copy(below, 2, 11 + j, at.at(at.z, at.ys(1), at.c)).start()
            self.wait(above, 7 + j)
            if j in (1, 2):
                self.copy(above, 2, 11 + j, at.at(at.z, at.ys(-1), at.c)).start()
        self.copy(self.line(at.ys(-1), at.c), 3, 16, at.sibling).start()
        self.copy(self.line(at.ys(1), at.c), 3, 17, at.sibling).start()

    def finish(self):
        at = self.at
        for j in (0, 1, 3, 2):
            self.wait(self.slot(at.zs(-j), at.ys(2), at.c), 11 + j)
        self.copy(self.line(at.ys(2), at.c), 3, 18, at.sibling).start()

    def settle(self):
        at = self.at
        for sem, step in ((15, 0), (16, -1), (17, 1), (18, 2)):
            self.wait(self.line(at.ys(step), 1 - at.c), sem)

    def drain(self):
        buf = self.buf
        for group, ref in enumerate((buf.at[0:3, 0, 0], buf.at[:, 0], buf.at[:, 0, 0], buf.at[:, :, 0])):
            self.copy(ref, group, 0, self.at.sibling).wait_send()


class Across:
    def __init__(self, at, buf, send, recv):
        self.at, self.buf, self.send, self.recv = at, buf, send, recv

    def line(self, x, step):
        return self.buf.at[x, :, self.at.ys(step), self.at.c]

    def copy(self, ref, group, sem, device):
        return remote(ref, ref, self.send.at[group], self.recv.at[sem], device)

    def start(self, *steps):
        at = self.at
        for step in steps:
            for i in (1, 3, 2):
                self.copy(self.line(at.x, step), 0, (step + 1) * 3 + i - 1, at.tensor_at(at.w, at.xs(i))).start()

    def swap(self):
        at = self.at
        for i in (1, 3, 2):
            for step in (0, -1, 1, 2):
                self.copy(self.line(at.xs(-i), step), 0, (step + 1) * 3 + i - 1, at.sibling).wait_recv()
            self.copy(self.buf.at[at.xs(-i), :, :, at.c], 1, 12 + i - 1, at.sibling).start()

    def settle(self):
        at = self.at
        for i in (1, 3, 2):
            self.copy(self.buf.at[at.xs(-i), :, :, 1 - at.c], 1, 12 + i - 1, at.sibling).wait_recv()

    def drain(self):
        for group in range(2):
            self.copy(self.buf.at[0:3, :, :, 0], group, 0, self.at.sibling).wait_send()


class Scatter:
    def __init__(self, at, part, from_x, total, from_w, x_send, x_recv, w_send, w_recv):
        self.at, self.part, self.from_x, self.total, self.from_w = at, part, from_x, total, from_w
        self.x_send, self.x_recv, self.w_send, self.w_recv = x_send, x_recv, w_send, w_recv

    def x_copy(self, j, i):
        at = self.at
        return remote(
            self.part.at[j, at.xs(i)], self.from_x.at[j, i - 1], self.x_send, self.x_recv.at[3 * j + i - 1],
            at.tensor_at(at.w, at.xs(i)),
        )

    def w_copy(self, j):
        at = self.at
        return remote(
            self.total.at[j - 1], self.from_w.at[j - 1], self.w_send, self.w_recv.at[j - 1],
            at.tensor_at(at.ws(-j), at.x),
        )

    def half_copy(self, h):
        at, lanes = self.at, pl.ds(h * (HALF // 2), HALF // 2)
        return remote(
            self.total.at[1, :, lanes], self.from_w.at[1, :, lanes], self.w_send, self.w_recv.at[3 if h else 1],
            at.tensor_at(at.ws(-1 if h else 1), at.x),
        )

    def fill(self, groups, left, matrix):
        for n in range(4):
            low, high = (
                times_transposed(left, row_block(matrix, m)).reshape(4 * len(groups), 8, 384) for m in (n, n + 4)
            )
            both = jnp.concatenate([low, high], axis=1).astype(BF16)
            for k, j in enumerate(groups):
                for x in range(4):
                    self.part[j, x, :, n * 384 : (n + 1) * 384] = both[4 * k + x]
        for j in groups:
            for i in (1, 3, 2):
                self.x_copy(j, i).start()

    def sum_x(self, j):
        total = self.part[j, self.at.x].astype(F32)
        for i in (1, 3, 2):
            self.x_copy(j, i).wait_recv()
            total = total + self.from_x[j, i - 1].astype(F32)
        return total

    def far(self):
        self.total[1] = self.sum_x(2).astype(BF16)
        for h in range(2):
            self.half_copy(h).start()

    def near(self, j):
        h = 1 if j == 1 else 0
        total = self.sum_x(j)
        self.half_copy(h).wait_recv()
        low, high = total[:, : HALF // 2], total[:, HALF // 2 :]
        half = self.from_w[1, :, h * (HALF // 2) : (h + 1) * (HALF // 2)].astype(F32)
        total = jnp.concatenate([low, high + half] if h else [low + half, high], axis=1)
        self.total[j - 1] = total.astype(BF16)
        self.w_copy(j).start()

    def done(self):
        total = self.sum_x(0)
        for j in (1, 3):
            self.w_copy(j).wait_recv()
            total = total + self.from_w[j - 1].astype(F32)
        return jnp.concatenate([total[0:8], total[8:16]], axis=1)

    def drain(self):
        at = self.at
        whole = self.part.at[0:3]
        remote(whole, whole, self.x_send, self.x_recv.at[0], at.sibling).wait_send()
        remote(self.total, self.total, self.w_send, self.w_recv.at[0], at.sibling).wait_send()


class Direct:
    def __init__(self, send, recv, peers):
        self.send, self.recv, self.peers = send, recv, peers

    def copy(self, j, src, dst):
        return remote(src, dst, self.send.at[j - 1], self.recv.at[j - 1], self.peers[j - 1])


class Lines:
    def __init__(self, at, buf, send, recv):
        self.at, self.buf, self.send, self.recv = at, buf, send, recv

    def copy(self, i, other=False):
        at = self.at
        ref = self.buf.at[at.ys(-i), 1 - at.c if other else at.c]
        return remote(ref, ref, self.send.at[3 + i], self.recv.at[3 + i], at.sibling)

    def along_y(self, i):
        at = self.at
        ref = self.buf.at[at.y, at.c]
        return remote(ref, ref, self.send.at[i - 1], self.recv.at[i - 1], at.y_peers()[i - 1])

    def start(self):
        for i in (2, 1, 3):
            self.along_y(i).start()
        self.copy(0).start()

    def middle(self):
        at = self.at
        for i in (1, 3, 2):
            ref = self.buf.at[at.ys(-i), at.c]
            remote(ref, ref, self.send.at[i - 1], self.recv.at[i - 1], at.sibling).wait_recv()
            self.copy(i).start()

    def settle(self):
        for i in (0, 1, 3, 2):
            self.copy(i, True).wait_recv()

    def drain(self):
        for i in (1, 2, 3):
            self.along_y(i).wait_send()
        for i in range(4):
            self.copy(i).wait_send()


class Spread:
    def __init__(self, at, buf, send, recv):
        self.at, self.buf, self.send, self.recv = at, buf, send, recv

    def copy(self, ref, group, sem, device):
        return remote(ref, ref, self.send.at[group], self.recv.at[sem], device)

    def along_x(self, j):
        at = self.at
        for i in (1, 3, 2):
            self.copy(self.buf.at[at.ws(-j), at.x], 1, 3 + 3 * j + i - 1, at.tensor_at(at.w, at.xs(i))).start()

    def start(self):
        at = self.at
        for j in (1, 3):
            self.copy(self.buf.at[at.w, at.x], 0, j - 1, at.tensor_at(at.ws(j), at.x)).start()
        self.along_x(0)

    def half(self, j, h):
        return self.buf.at[self.at.ws(-j), self.at.x, :, pl.ds(h * (HALF // 2), HALF // 2)]

    def forward(self, j):
        at = self.at
        if j == 2:
            self.copy(self.half(2, 0), 0, 1, at.sibling).wait_recv()
            self.copy(self.half(2, 1), 0, 15, at.sibling).wait_recv()
        else:
            self.copy(self.buf.at[at.ws(-j), at.x], 0, j - 1, at.sibling).wait_recv()
            h = 0 if j == 1 else 1
            self.copy(self.half(j, h), 0, 15 if h else 1, at.tensor_at(at.ws(j), at.x)).start()
        self.along_x(j)

    def settle(self, j):
        at = self.at
        for i in (1, 3, 2):
            self.copy(self.buf.at[at.ws(-j), at.xs(-i)], 1, 3 + 3 * j + i - 1, at.sibling).wait_recv()

    def drain(self):
        self.copy(self.buf.at[0:3, 0], 0, 0, self.at.sibling).wait_send()
        self.copy(self.buf.at[0:3], 1, 0, self.at.sibling).wait_send()


def row_block(matrix, n):
    y = 2 * (n % 2)
    return matrix[n // 2, y : y + 2].reshape(384, matrix.shape[-1])


def row_pair(ref, tensor):
    return ref.at[pl.ds(pl.multiple_of((tensor // 2) * 16, 16), 16), :]


def own_rows(pair, tensor):
    pair = pair.astype(F32)
    return jnp.where(lax.rem(tensor, 2) == 0, pair[0:8], pair[8:16])


def kernel(
    control_in, control_project, control_output, query_gain, key_gain, base_hidden, base_up, base_down, cotangent,
    base_out, feat_grad,
    w_buf, kv_buf, q_buf, co_buf, up_buf, down_buf, own_in, own_gain, own_base, own_cot,
    normed_in, scores, stat, stat_back, mix32, mix16, mix_back, mix_send, mix_recv, feat32, feat16, feat_recv, spread_buf, normed, hidden_grad,
    part, from_x, total, from_w,
    local_sem, gather_send, gather_recv, kv_send, kv_recv, across_send, across_recv, direct_send, direct_recv,
    x_send, x_recv, w_send, w_recv, spread_send, spread_recv,
):
    at = Place()
    barrier = pltpu.get_barrier_semaphore()
    partners = at.partners()
    for device in partners:
        pl.semaphore_signal(barrier, inc=1, device_id=device, device_id_type=MESH)

    project, co, up, down = (
        Gather(at, buf, gather_send.at[i], gather_recv.at[i])
        for i, buf in enumerate((w_buf, co_buf.at[at.x], up_buf, down_buf))
    )
    kv = Lines(at, kv_buf, kv_send, kv_recv)
    ask = Direct(direct_send.at[2], direct_recv.at[2], at.z_peers())
    answer = Direct(direct_send.at[3], direct_recv.at[3], at.z_peers())
    answer_stat = Direct(direct_send.at[4], direct_recv.at[4], at.z_peers())
    co_x = Across(at, co_buf, across_send, across_recv)
    added, grad = (
        Scatter(at, *(ref.at[i] for ref in (part, from_x, total, from_w, x_send, x_recv, w_send, w_recv)))
        for i in range(2)
    )
    spread = Spread(at, spread_buf, spread_send, spread_recv)
    heads = Direct(direct_send.at[0], direct_recv.at[0], at.x_peers())
    feats = Direct(direct_send.at[1], direct_recv.at[1], at.w_peers())

    def own(gather):
        return gather.slot(at.z, at.y, at.c)

    loads = [
        pltpu.make_async_copy(src, dst, local_sem.at[i])
        for i, (src, dst) in enumerate(
            (
                (control_project.at[0], own(project).at[:, 0:128]),
                (control_project.at[1], own(project).at[:, 128:256]),
                (control_project.at[2], own(project).at[:, 256:384]),
                (control_in, own_in),
                (control_output, own(co)),
                (query_gain, own_gain.at[0]),
                (key_gain, own_gain.at[1]),
                (base_up, own(up)),
                (base_down, own(down)),
                (row_pair(base_hidden, at.tensor), own_base),
                (cotangent, own_cot),
            )
        )
    ]
    for load in loads:
        load.start()
    pl.semaphore_wait(barrier, len(partners))

    for load in loads[0:3]:
        load.wait()
    project.start()
    project.both_ways(0)
    loads[3].wait()
    normed_in[...] = norm_rows(own_in[...].astype(F32))[0].astype(BF16)
    project.middle(False)
    for load in loads[4:]:
        load.wait()
    co.start()
    project.relay()
    co.middle()
    co_x.start(0)
    up.start()
    down.start()
    project.finish()
    co.relay()
    co_x.start(-1, 1)
    project.settle()
    projected = jnp.dot(normed_in[...], w_buf[...].reshape(D, 384), preferred_element_type=F32)
    kv_buf[at.y, at.c, :, 0:128] = head_norm(projected[:, 128:256], own_gain[1])
    kv_buf[at.y, at.c, :, 128:256] = projected[:, 256:384].astype(BF16)
    kv.start()
    q_buf[at.z] = head_norm(projected[:, 0:128], own_gain[0])
    for j in (2, 1, 3):
        ask.copy(j, q_buf.at[at.z], q_buf.at[at.z]).start()
    kv.middle()
    co.finish()
    co_x.start(2)
    up.middle()
    for j in (1, 3, 2):
        ask.copy(j, q_buf.at[at.z], q_buf.at[at.zs(-j)]).wait_recv()
    kv.settle()
    asked = q_buf[...].reshape(512, 128)
    for y in range(4):
        block = kv_buf[y].reshape(256, 256)[:, 0:128]
        scores[y * 256 : (y + 1) * 256, :] = times_transposed(block, asked) * (1.0 / 128**0.5)
    values = kv_buf[...].reshape(1024, 256)[:, 128:256]
    for z in range(4):
        block = scores[:, z * 128 : (z + 1) * 128]
        top = jnp.max(block, axis=0, keepdims=True)
        expo = jnp.exp(block - top)
        sums = jnp.sum(expo, axis=0, keepdims=True)
        stat[z] = jnp.concatenate([top, sums, jnp.zeros((6, 128), F32)], axis=0)
        accum = lax.dot_general(
            values, expo.astype(BF16), (((0,), (0,)), ((), ())), preferred_element_type=F32
        )
        mix32[z] = accum
        mix16[z] = accum.astype(BF16)
    for j in (2, 1, 3):
        answer.copy(j, mix16.at[at.zs(j)], mix_back.at[j - 1]).start()
        answer_stat.copy(j, stat.at[at.zs(j)], stat_back.at[j - 1]).start()
    co.settle()
    co_x.swap()
    down.middle()
    accums, stats = [mix32[at.z]], [stat[at.z]]
    for j in (1, 3, 2):
        answer.copy(j, mix16.at[at.zs(j)], mix_back.at[j - 1]).wait_recv()
        answer_stat.copy(j, stat.at[at.zs(j)], stat_back.at[j - 1]).wait_recv()
        accums.append(mix_back[j - 1].astype(F32))
        stats.append(stat_back[j - 1])
    top = functools.reduce(jnp.maximum, [each[0:1] for each in stats])
    shares = [jnp.exp(each[0:1] - top) for each in stats]
    row_sum = sum(share * each[1:2] for share, each in zip(shares, stats))
    mixed = sum(share * each for share, each in zip(shares, accums)) / row_sum
    mixed = jnp.transpose(mixed).reshape(4, 4, 8, 128)
    for x in range(4):
        mix_send[x] = mixed[:, x].reshape(32, 128).astype(BF16)
    for j in (1, 3, 2):
        heads.copy(j, mix_send.at[at.xs(j)], mix_recv.at[at.x]).start()
    mix_recv[at.x] = mix_send[at.x]
    up.relay()
    co_x.settle()
    for j in (1, 3, 2):
        heads.copy(j, mix_send.at[at.xs(j)], mix_recv.at[at.xs(-j)]).wait_recv()
    mixed = jnp.concatenate([mix_recv[x] for x in range(4)], axis=1)
    for n in range(4):
        low, high = (
            times_transposed(
                mixed, jnp.concatenate([row_block(co_buf.at[x], m) for x in range(4)], axis=1)
            ).reshape(4, 8, 384)
            for m in (n, n + 4)
        )
        both = jnp.concatenate([low, high], axis=1)
        feat32[:, :, n * 384 : (n + 1) * 384] = both
        feat16[:, :, n * 384 : (n + 1) * 384] = both.astype(BF16)
    for j in (2, 1, 3):
        feats.copy(j, feat16.at[at.ws(j)], feat_recv.at[j - 1]).start()
    down.relay()
    up.finish()
    down.finish()
    feat = feat32[at.w]
    for j in (1, 3, 2):
        feats.copy(j, feat16.at[at.ws(j)], feat_recv.at[j - 1]).wait_recv()
        feat = feat + feat_recv[j - 1].astype(F32)
    summed = own_rows(own_base[...], at.tensor) + jnp.concatenate([feat[0:8], feat[8:16]], axis=1)
    nhat, rstd = norm_rows(summed)
    spread_buf[at.w, at.x] = jnp.concatenate([nhat[:, :HALF], nhat[:, HALF:]], axis=0).astype(BF16)
    spread.start()
    up.settle()
    down.settle()
    hidden_grad[...] = jnp.dot(
        own_cot[...], down_buf[...].reshape(D, 384), preferred_element_type=F32
    ).reshape(4, 32, 384)

    def mlp(*groups):
        for j in groups:
            spread.settle(j)
            w = at.ws(-j)
            blocks = [spread_buf[w, x].astype(F32) for x in range(4)]
            for k in (0, 2):
                for h in range(2):
                    normed[j, k * 8 : k * 8 + 16, h * HALF : (h + 1) * HALF] = jnp.concatenate(
                        [block[h * 8 : (h + 1) * 8] for block in blocks[k : k + 2]], axis=0
                    ).astype(BF16)
        pre = jnp.dot(
            jnp.concatenate([normed[j] for j in groups], axis=0), up_buf[...].reshape(D, 384), preferred_element_type=F32
        )
        tangent = jnp.tanh(0.7978845608028654 * (pre + 0.044715 * pre * pre * pre))
        hidden = (0.5 * pre * (1.0 + tangent)).astype(BF16)
        slope = 0.5 * (1.0 + tangent) + 0.5 * pre * (1.0 - tangent * tangent) * 0.7978845608028654 * (
            1.0 + 3.0 * 0.044715 * pre * pre
        )
        arriving = jnp.concatenate([hidden_grad[at.ws(-j)] for j in groups], axis=0)
        added.fill(groups, hidden, down_buf)
        grad.fill(groups, (arriving * slope).astype(BF16), up_buf)

    mlp(0)
    spread.forward(1)
    spread.forward(3)
    spread.forward(2)
    mlp(2)
    mlp(1, 3)
    added.far()
    grad.far()
    for j in (1, 3):
        added.near(j)
    for j in (1, 3):
        grad.near(j)
    base_out[...] = summed + added.done()
    normed_grad = grad.done()
    feat_grad[...] = own_rows(row_pair(own_cot, at.tensor)[...], at.tensor) + rstd * (
        normed_grad
        - jnp.mean(normed_grad, axis=-1, keepdims=True)
        - nhat * jnp.mean(normed_grad * nhat, axis=-1, keepdims=True)
    )
    for each in (project, kv, co, up, down, co_x, spread, added, grad):
        each.drain()
    for j in (1, 2, 3):
        ask.copy(j, q_buf.at[at.z], q_buf.at[at.z]).wait_send()
        answer.copy(j, mix16.at[at.zs(j)], mix_back.at[j - 1]).wait_send()
        answer_stat.copy(j, stat.at[at.zs(j)], stat_back.at[j - 1]).wait_send()
        heads.copy(j, mix_send.at[at.xs(j)], mix_recv.at[at.x]).wait_send()
        feats.copy(j, feat16.at[at.ws(j)], feat_recv.at[j - 1]).wait_send()


def body(*args):
    args = list(args)
    args[3] = args[3].reshape(1, 128)
    args[4] = args[4].reshape(1, 128)
    vmem = pl.BlockSpec(memory_space=pltpu.VMEM)
    out = pl.pallas_call(
        kernel,
        out_shape=[jax.ShapeDtypeStruct((8, D), F32)] * 2,
        in_specs=[pl.BlockSpec(memory_space=pltpu.HBM)] * 9,
        out_specs=[vmem] * 2,
        scratch_shapes=[
            pltpu.VMEM((4, 4, 2, 96, 384), BF16),
            pltpu.VMEM((4, 2, 128, 256), BF16),
            pltpu.VMEM((4, 128, 128), BF16),
            pltpu.VMEM((4, 4, 4, 2, 96, 128), BF16),
            pltpu.VMEM((4, 4, 2, 96, 384), BF16),
            pltpu.VMEM((4, 4, 2, 96, 384), BF16),
            pltpu.VMEM((128, D), BF16),
            pltpu.VMEM((2, 1, 128), F32),
            pltpu.VMEM((16, D), BF16),
            pltpu.VMEM((128, D), BF16),
            pltpu.VMEM((128, D), BF16),
            pltpu.VMEM((1024, 512), F32),
            pltpu.VMEM((4, 8, 128), F32),
            pltpu.VMEM((3, 8, 128), F32),
            pltpu.VMEM((4, 128, 128), F32),
            pltpu.VMEM((4, 128, 128), BF16),
            pltpu.VMEM((3, 128, 128), BF16),
            pltpu.VMEM((4, 32, 128), BF16),
            pltpu.VMEM((4, 32, 128), BF16),
            pltpu.VMEM((4, 16, HALF), F32),
            pltpu.VMEM((4, 16, HALF), BF16),
            pltpu.VMEM((3, 16, HALF), BF16),
            pltpu.VMEM((4, 4, 16, HALF), BF16),
            pltpu.VMEM((4, 32, D), BF16),
            pltpu.VMEM((4, 32, 384), F32),
            pltpu.VMEM((2, 4, 4, 16, HALF), BF16),
            pltpu.VMEM((2, 4, 3, 16, HALF), BF16),
            pltpu.VMEM((2, 3, 16, HALF), BF16),
            pltpu.VMEM((2, 3, 16, HALF), BF16),
            pltpu.SemaphoreType.DMA((11,)),
            pltpu.SemaphoreType.DMA((4, 4)),
            pltpu.SemaphoreType.DMA((4, 19)),
            pltpu.SemaphoreType.DMA((7,)),
            pltpu.SemaphoreType.DMA((7,)),
            pltpu.SemaphoreType.DMA((2,)),
            pltpu.SemaphoreType.DMA((15,)),
            pltpu.SemaphoreType.DMA((5, 3)),
            pltpu.SemaphoreType.DMA((5, 3)),
            pltpu.SemaphoreType.DMA((2,)),
            pltpu.SemaphoreType.DMA((2, 12)),
            pltpu.SemaphoreType.DMA((2,)),
            pltpu.SemaphoreType.DMA((2, 4)),
            pltpu.SemaphoreType.DMA((2,)),
            pltpu.SemaphoreType.DMA((16,)),
        ],
        compiler_params=pltpu.CompilerParams(
            collective_id=0, has_side_effects=True, vmem_limit_bytes=64000 * 1024
        ),
    )(*args)
    return tuple(each.astype(BF16) for each in out)


def solution(mesh):
    placed = (
        P("dp", None),
        P(None, "dp", "tensor"),
        P("dp", "tensor"),
        P(),
        P(),
        P("dp", None),
        P("dp", "tensor"),
        P("dp", "tensor"),
        P("dp", None),
    )
    return jax.shard_map(
        body,
        mesh=mesh,
        in_specs=placed,
        out_specs=(P(("dp", "tensor"), None), P(("dp", "tensor"), None)),
        check_vma=False,
    )
```

```python
import functools

import jax
import jax.numpy as jnp
from jax import lax
from jax.experimental import pallas as pl
from jax.experimental.pallas import tpu as pltpu
from jax.sharding import PartitionSpec as P

F32 = jnp.float32
BF16 = jnp.bfloat16
MESH = pl.DeviceIdType.MESH
D = 3072
HALF = D // 2


def norm_rows(values):
    center = values - jnp.mean(values, axis=-1, keepdims=True)
    spread = jnp.mean(center * center, axis=-1, keepdims=True)
    rstd = lax.rsqrt(spread + 1e-06)
    return (center * rstd, rstd)


def head_norm(values, gain):
    square_mean = jnp.mean(values * values, axis=-1, keepdims=True)
    return (values * lax.rsqrt(square_mean + 1e-06) * gain).astype(BF16)


def times_transposed(left, right):
    return lax.dot_general(left, right, (((1,), (1,)), ((), ())), preferred_element_type=F32)


class Place:
    def __init__(self):
        dp, tensor = lax.axis_index("dp"), lax.axis_index("tensor")
        self.dp, self.tensor = dp, tensor
        self.z, self.y, self.c = dp // 8, lax.rem(dp // 2, 4), lax.rem(dp, 2)
        self.w, self.x = tensor // 4, lax.rem(tensor, 4)
        self.sibling = self.at(self.z, self.y, 1 - self.c)

    def at(self, z, y, c):
        return (z * 8 + y * 2 + c, self.tensor)

    def zs(self, j):
        return lax.rem(self.z + (j + 4), 4)

    def ys(self, j):
        return lax.rem(self.y + (j + 4), 4)

    def xs(self, j):
        return lax.rem(self.x + (j + 4), 4)

    def ws(self, j):
        return lax.rem(self.w + (j + 4), 4)

    def tensor_at(self, w, x):
        return (self.dp, w * 4 + x)

    def partners(self):
        return (
            self.z_peers()
            + self.y_peers()
            + [self.sibling]
            + self.x_peers()
            + self.w_peers()
        )

    def z_peers(self):
        return [self.at(self.zs(j), self.y, self.c) for j in (1, 2, 3)]

    def y_peers(self):
        return [self.at(self.z, self.ys(j), self.c) for j in (1, 2, 3)]

    def x_peers(self):
        return [self.tensor_at(self.w, self.xs(j)) for j in (1, 2, 3)]

    def w_peers(self):
        return [self.tensor_at(self.ws(j), self.x) for j in (1, 2, 3)]


def remote(src, dst, send, recv, device):
    return pltpu.make_async_remote_copy(
        src_ref=src, dst_ref=dst, send_sem=send, recv_sem=recv, device_id=device, device_id_type=MESH
    )


class Gather:
    def __init__(self, at, buf, send, recv):
        self.at, self.buf, self.send, self.recv = at, buf, send, recv

    def slot(self, z, y, c):
        return self.buf.at[z, y, c]

    def line(self, y, c):
        return self.buf.at[:, y, c]

    def copy(self, ref, group, sem, device):
        return remote(ref, ref, self.send.at[group], self.recv.at[sem], device)

    def wait(self, ref, sem):
        self.copy(ref, 0, sem, self.at.sibling).wait_recv()

    def both_ways(self, j):
        at = self.at
        ref = self.slot(at.zs(-j), at.y, at.c)
        self.copy(ref, 1, 3 + j, at.at(at.z, at.ys(1), at.c)).start()
        self.copy(ref, 1, 7 + j, at.at(at.z, at.ys(-1), at.c)).start()

    def start(self):
        at = self.at
        for j in (1, 3, 2):
            self.copy(self.slot(at.z, at.y, at.c), 0, j - 1, at.at(at.zs(j), at.y, at.c)).start()

    def middle(self, own=True):
        at = self.at
        if own:
            self.both_ways(0)
        for j in (1, 3, 2):
            self.wait(self.slot(at.zs(-j), at.y, at.c), j - 1)
            self.both_ways(j)
        self.copy(self.line(at.y, at.c), 3, 15, at.sibling).start()

    def relay(self):
        at = self.at
        for j in (0, 1, 3, 2):
            below, above = self.slot(at.zs(-j), at.ys(-1), at.c), self.slot(at.zs(-j), at.ys(1), at.c)
            self.wait(below, 3 + j)
            if j in (0, 3):
                self.copy(below, 2, 11 + j, at.at(at.z, at.ys(1), at.c)).start()
            self.wait(above, 7 + j)
            if j in (1, 2):
                self.copy(above, 2, 11 + j, at.at(at.z, at.ys(-1), at.c)).start()
        self.copy(self.line(at.ys(-1), at.c), 3, 16, at.sibling).start()
        self.copy(self.line(at.ys(1), at.c), 3, 17, at.sibling).start()

    def finish(self):
        at = self.at
        for j in (0, 1, 3, 2):
            self.wait(self.slot(at.zs(-j), at.ys(2), at.c), 11 + j)
        self.copy(self.line(at.ys(2), at.c), 3, 18, at.sibling).start()

    def settle(self):
        at = self.at
        for sem, step in ((15, 0), (16, -1), (17, 1), (18, 2)):
            self.wait(self.line(at.ys(step), 1 - at.c), sem)

    def drain(self):
        buf = self.buf
        for group, ref in enumerate((buf.at[0:3, 0, 0], buf.at[:, 0], buf.at[:, 0, 0], buf.at[:, :, 0])):
            self.copy(ref, group, 0, self.at.sibling).wait_send()


class Across:
    def __init__(self, at, buf, send, recv):
        self.at, self.buf, self.send, self.recv = at, buf, send, recv

    def line(self, x, step):
        return self.buf.at[x, :, self.at.ys(step), self.at.c]

    def copy(self, ref, group, sem, device):
        return remote(ref, ref, self.send.at[group], self.recv.at[sem], device)

    def start(self, *steps):
        at = self.at
        for step in steps:
            for i in (1, 3, 2):
                self.copy(self.line(at.x, step), 0, (step + 1) * 3 + i - 1, at.tensor_at(at.w, at.xs(i))).start()

    def swap(self):
        at = self.at
        for i in (1, 3, 2):
            for step in (0, -1, 1, 2):
                self.copy(self.line(at.xs(-i), step), 0, (step + 1) * 3 + i - 1, at.sibling).wait_recv()
            self.copy(self.buf.at[at.xs(-i), :, :, at.c], 1, 12 + i - 1, at.sibling).start()

    def settle(self):
        at = self.at
        for i in (1, 3, 2):
            self.copy(self.buf.at[at.xs(-i), :, :, 1 - at.c], 1, 12 + i - 1, at.sibling).wait_recv()

    def drain(self):
        for group in range(2):
            self.copy(self.buf.at[0:3, :, :, 0], group, 0, self.at.sibling).wait_send()


class Scatter:
    def __init__(self, at, part, from_x, total, from_w, x_send, x_recv, w_send, w_recv):
        self.at, self.part, self.from_x, self.total, self.from_w = at, part, from_x, total, from_w
        self.x_send, self.x_recv, self.w_send, self.w_recv = x_send, x_recv, w_send, w_recv

    def x_copy(self, j, i):
        at = self.at
        return remote(
            self.part.at[j, at.xs(i)], self.from_x.at[j, i - 1], self.x_send, self.x_recv.at[3 * j + i - 1],
            at.tensor_at(at.w, at.xs(i)),
        )

    def w_copy(self, j):
        at = self.at
        return remote(
            self.total.at[j - 1], self.from_w.at[j - 1], self.w_send, self.w_recv.at[j - 1],
            at.tensor_at(at.ws(-j), at.x),
        )

    def half_copy(self, h):
        at, lanes = self.at, pl.ds(h * (HALF // 2), HALF // 2)
        return remote(
            self.total.at[1, :, lanes], self.from_w.at[1, :, lanes], self.w_send, self.w_recv.at[3 if h else 1],
            at.tensor_at(at.ws(-1 if h else 1), at.x),
        )

    def fill(self, groups, left, matrix):
        for n in range(4):
            low, high = (
                times_transposed(left, row_block(matrix, m)).reshape(4 * len(groups), 8, 384) for m in (n, n + 4)
            )
            both = jnp.concatenate([low, high], axis=1).astype(BF16)
            for k, j in enumerate(groups):
                for x in range(4):
                    self.part[j, x, :, n * 384 : (n + 1) * 384] = both[4 * k + x]
        for j in groups:
            for i in (1, 3, 2):
                self.x_copy(j, i).start()

    def sum_x(self, j):
        total = self.part[j, self.at.x].astype(F32)
        for i in (1, 3, 2):
            self.x_copy(j, i).wait_recv()
            total = total + self.from_x[j, i - 1].astype(F32)
        return total

    def far(self):
        self.total[1] = self.sum_x(2).astype(BF16)
        for h in range(2):
            self.half_copy(h).start()

    def near(self, j):
        h = 1 if j == 1 else 0
        total = self.sum_x(j)
        self.half_copy(h).wait_recv()
        low, high = total[:, : HALF // 2], total[:, HALF // 2 :]
        half = self.from_w[1, :, h * (HALF // 2) : (h + 1) * (HALF // 2)].astype(F32)
        total = jnp.concatenate([low, high + half] if h else [low + half, high], axis=1)
        self.total[j - 1] = total.astype(BF16)
        self.w_copy(j).start()

    def done(self):
        total = self.sum_x(0)
        for j in (1, 3):
            self.w_copy(j).wait_recv()
            total = total + self.from_w[j - 1].astype(F32)
        return jnp.concatenate([total[0:8], total[8:16]], axis=1)

    def drain(self):
        at = self.at
        whole = self.part.at[0:3]
        remote(whole, whole, self.x_send, self.x_recv.at[0], at.sibling).wait_send()
        remote(self.total, self.total, self.w_send, self.w_recv.at[0], at.sibling).wait_send()


class Direct:
    def __init__(self, send, recv, peers):
        self.send, self.recv, self.peers = send, recv, peers

    def copy(self, j, src, dst):
        return remote(src, dst, self.send.at[j - 1], self.recv.at[j - 1], self.peers[j - 1])


class Lines:
    def __init__(self, at, buf, send, recv):
        self.at, self.buf, self.send, self.recv = at, buf, send, recv

    def copy(self, i, other=False):
        at = self.at
        ref = self.buf.at[at.ys(-i), 1 - at.c if other else at.c]
        return remote(ref, ref, self.send.at[3 + i], self.recv.at[3 + i], at.sibling)

    def along_y(self, i):
        at = self.at
        ref = self.buf.at[at.y, at.c]
        return remote(ref, ref, self.send.at[i - 1], self.recv.at[i - 1], at.y_peers()[i - 1])

    def start(self):
        for i in (2, 1, 3):
            self.along_y(i).start()
        self.copy(0).start()

    def middle(self):
        at = self.at
        for i in (1, 3, 2):
            ref = self.buf.at[at.ys(-i), at.c]
            remote(ref, ref, self.send.at[i - 1], self.recv.at[i - 1], at.sibling).wait_recv()
            self.copy(i).start()

    def settle(self):
        for i in (0, 1, 3, 2):
            self.copy(i, True).wait_recv()

    def drain(self):
        for i in (1, 2, 3):
            self.along_y(i).wait_send()
        for i in range(4):
            self.copy(i).wait_send()


class Spread:
    def __init__(self, at, buf, send, recv):
        self.at, self.buf, self.send, self.recv = at, buf, send, recv

    def copy(self, ref, group, sem, device):
        return remote(ref, ref, self.send.at[group], self.recv.at[sem], device)

    def along_x(self, j):
        at = self.at
        for i in (1, 3, 2):
            self.copy(self.buf.at[at.ws(-j), at.x], 1, 3 + 3 * j + i - 1, at.tensor_at(at.w, at.xs(i))).start()

    def start(self):
        at = self.at
        for j in (1, 3):
            self.copy(self.buf.at[at.w, at.x], 0, j - 1, at.tensor_at(at.ws(j), at.x)).start()
        self.along_x(0)

    def half(self, j, h):
        return self.buf.at[self.at.ws(-j), self.at.x, :, pl.ds(h * (HALF // 2), HALF // 2)]

    def forward(self, j):
        at = self.at
        if j == 2:
            self.copy(self.half(2, 0), 0, 1, at.sibling).wait_recv()
            self.copy(self.half(2, 1), 0, 15, at.sibling).wait_recv()
        else:
            self.copy(self.buf.at[at.ws(-j), at.x], 0, j - 1, at.sibling).wait_recv()
            h = 0 if j == 1 else 1
            self.copy(self.half(j, h), 0, 15 if h else 1, at.tensor_at(at.ws(j), at.x)).start()
        self.along_x(j)

    def settle(self, j):
        at = self.at
        for i in (1, 3, 2):
            self.copy(self.buf.at[at.ws(-j), at.xs(-i)], 1, 3 + 3 * j + i - 1, at.sibling).wait_recv()

    def drain(self):
        self.copy(self.buf.at[0:3, 0], 0, 0, self.at.sibling).wait_send()
        self.copy(self.buf.at[0:3], 1, 0, self.at.sibling).wait_send()


def row_block(matrix, n):
    y = 2 * (n % 2)
    return matrix[n // 2, y : y + 2].reshape(384, matrix.shape[-1])


def row_pair(ref, tensor):
    return ref.at[pl.ds(pl.multiple_of((tensor // 2) * 16, 16), 16), :]


def own_rows(pair, tensor):
    pair = pair.astype(F32)
    return jnp.where(lax.rem(tensor, 2) == 0, pair[0:8], pair[8:16])


def kernel(
    control_in, control_project, control_output, query_gain, key_gain, base_hidden, base_up, base_down, cotangent,
    base_out, feat_grad,
    w_buf, kv_buf, q_buf, co_buf, up_buf, down_buf, own_in, own_gain, own_base, own_cot,
    normed_in, scores, stat, stat_back, mix32, mix16, mix_back, mix_send, mix_recv, feat32, feat16, feat_recv, spread_buf, normed, hidden_grad,
    part, from_x, total, from_w,
    local_sem, gather_send, gather_recv, kv_send, kv_recv, across_send, across_recv, direct_send, direct_recv,
    x_send, x_recv, w_send, w_recv, spread_send, spread_recv,
):
    at = Place()
    barrier = pltpu.get_barrier_semaphore()
    partners = at.partners()
    for device in partners:
        pl.semaphore_signal(barrier, inc=1, device_id=device, device_id_type=MESH)

    project, co, up, down = (
        Gather(at, buf, gather_send.at[i], gather_recv.at[i])
        for i, buf in enumerate((w_buf, co_buf.at[at.x], up_buf, down_buf))
    )
    kv = Lines(at, kv_buf, kv_send, kv_recv)
    ask = Direct(direct_send.at[2], direct_recv.at[2], at.z_peers())
    answer = Direct(direct_send.at[3], direct_recv.at[3], at.z_peers())
    answer_stat = Direct(direct_send.at[4], direct_recv.at[4], at.z_peers())
    co_x = Across(at, co_buf, across_send, across_recv)
    added, grad = (
        Scatter(at, *(ref.at[i] for ref in (part, from_x, total, from_w, x_send, x_recv, w_send, w_recv)))
        for i in range(2)
    )
    spread = Spread(at, spread_buf, spread_send, spread_recv)
    heads = Direct(direct_send.at[0], direct_recv.at[0], at.x_peers())
    feats = Direct(direct_send.at[1], direct_recv.at[1], at.w_peers())

    def own(gather):
        return gather.slot(at.z, at.y, at.c)

    loads = [
        pltpu.make_async_copy(src, dst, local_sem.at[i])
        for i, (src, dst) in enumerate(
            (
                (control_project.at[0], own(project).at[:, 0:128]),
                (control_project.at[1], own(project).at[:, 128:256]),
                (control_project.at[2], own(project).at[:, 256:384]),
                (control_in, own_in),
                (control_output, own(co)),
                (query_gain, own_gain.at[0]),
                (key_gain, own_gain.at[1]),
                (base_up, own(up)),
                (base_down, own(down)),
                (row_pair(base_hidden, at.tensor), own_base),
                (cotangent, own_cot),
            )
        )
    ]
    for load in loads:
        load.start()
    pl.semaphore_wait(barrier, len(partners))

    for load in loads[0:3]:
        load.wait()
    project.start()
    project.both_ways(0)
    loads[3].wait()
    normed_in[...] = norm_rows(own_in[...].astype(F32))[0].astype(BF16)
    project.middle(False)
    for load in loads[4:]:
        load.wait()
    co.start()
    project.relay()
    co.middle()
    co_x.start(0)
    up.start()
    down.start()
    project.finish()
    co.relay()
    co_x.start(-1, 1)
    project.settle()
    projected = jnp.dot(normed_in[...], w_buf[...].reshape(D, 384), preferred_element_type=F32)
    kv_buf[at.y, at.c, :, 0:128] = head_norm(projected[:, 128:256], own_gain[1])
    kv_buf[at.y, at.c, :, 128:256] = projected[:, 256:384].astype(BF16)
    kv.start()
    q_buf[at.z] = head_norm(projected[:, 0:128], own_gain[0])
    for j in (2, 1, 3):
        ask.copy(j, q_buf.at[at.z], q_buf.at[at.z]).start()
    kv.middle()
    co.finish()
    co_x.start(2)
    up.middle()
    for j in (1, 3, 2):
        ask.copy(j, q_buf.at[at.z], q_buf.at[at.zs(-j)]).wait_recv()
    kv.settle()
    asked = q_buf[...].reshape(512, 128)
    for y in range(4):
        block = kv_buf[y].reshape(256, 256)[:, 0:128]
        scores[y * 256 : (y + 1) * 256, :] = times_transposed(block, asked) * (1.0 / 128**0.5)
    values = kv_buf[...].reshape(1024, 256)[:, 128:256]
    for z in range(4):
        block = scores[:, z * 128 : (z + 1) * 128]
        top = jnp.max(block, axis=0, keepdims=True)
        expo = jnp.exp(block - top)
        sums = jnp.sum(expo, axis=0, keepdims=True)
        stat[z] = jnp.concatenate([top, sums, jnp.zeros((6, 128), F32)], axis=0)
        accum = lax.dot_general(
            values, expo.astype(BF16), (((0,), (0,)), ((), ())), preferred_element_type=F32
        )
        mix32[z] = accum
        mix16[z] = accum.astype(BF16)
    for j in (2, 1, 3):
        answer.copy(j, mix16.at[at.zs(j)], mix_back.at[j - 1]).start()
        answer_stat.copy(j, stat.at[at.zs(j)], stat_back.at[j - 1]).start()
    co.settle()
    co_x.swap()
    down.middle()
    accums, stats = [mix32[at.z]], [stat[at.z]]
    for j in (1, 3, 2):
        answer.copy(j, mix16.at[at.zs(j)], mix_back.at[j - 1]).wait_recv()
        answer_stat.copy(j, stat.at[at.zs(j)], stat_back.at[j - 1]).wait_recv()
        accums.append(mix_back[j - 1].astype(F32))
        stats.append(stat_back[j - 1])
    top = functools.reduce(jnp.maximum, [each[0:1] for each in stats])
    shares = [jnp.exp(each[0:1] - top) for each in stats]
    row_sum = sum(share * each[1:2] for share, each in zip(shares, stats))
    mixed = sum(share * each for share, each in zip(shares, accums)) / row_sum
    mixed = jnp.transpose(mixed).reshape(4, 4, 8, 128)
    for x in range(4):
        mix_send[x] = mixed[:, x].reshape(32, 128).astype(BF16)
    for j in (1, 3, 2):
        heads.copy(j, mix_send.at[at.xs(j)], mix_recv.at[at.x]).start()
    mix_recv[at.x] = mix_send[at.x]
    up.relay()
    co_x.settle()
    for j in (1, 3, 2):
        heads.copy(j, mix_send.at[at.xs(j)], mix_recv.at[at.xs(-j)]).wait_recv()
    mixed = jnp.concatenate([mix_recv[x] for x in range(4)], axis=1)
    for n in range(4):
        low, high = (
            times_transposed(
                mixed, jnp.concatenate([row_block(co_buf.at[x], m) for x in range(4)], axis=1)
            ).reshape(4, 8, 384)
            for m in (n, n + 4)
        )
        both = jnp.concatenate([low, high], axis=1)
        feat32[:, :, n * 384 : (n + 1) * 384] = both
        feat16[:, :, n * 384 : (n + 1) * 384] = both.astype(BF16)
    for j in (2, 1, 3):
        feats.copy(j, feat16.at[at.ws(j)], feat_recv.at[j - 1]).start()
    down.relay()
    up.finish()
    down.finish()
    feat = feat32[at.w]
    for j in (1, 3, 2):
        feats.copy(j, feat16.at[at.ws(j)], feat_recv.at[j - 1]).wait_recv()
        feat = feat + feat_recv[j - 1].astype(F32)
    summed = own_rows(own_base[...], at.tensor) + jnp.concatenate([feat[0:8], feat[8:16]], axis=1)
    nhat, rstd = norm_rows(summed)
    spread_buf[at.w, at.x] = jnp.concatenate([nhat[:, :HALF], nhat[:, HALF:]], axis=0).astype(BF16)
    spread.start()
    spread.forward(1)
    spread.forward(3)
    up.settle()
    down.settle()
    hidden_grad[...] = jnp.dot(
        own_cot[...], down_buf[...].reshape(D, 384), preferred_element_type=F32
    ).reshape(4, 32, 384)

    def mlp(*groups):
        for j in groups:
            spread.settle(j)
            w = at.ws(-j)
            blocks = [spread_buf[w, x].astype(F32) for x in range(4)]
            for k in (0, 2):
                for h in range(2):
                    normed[j, k * 8 : k * 8 + 16, h * HALF : (h + 1) * HALF] = jnp.concatenate(
                        [block[h * 8 : (h + 1) * 8] for block in blocks[k : k + 2]], axis=0
                    ).astype(BF16)
        pre = jnp.dot(
            jnp.concatenate([normed[j] for j in groups], axis=0), up_buf[...].reshape(D, 384), preferred_element_type=F32
        )
        tangent = jnp.tanh(0.7978845608028654 * (pre + 0.044715 * pre * pre * pre))
        hidden = (0.5 * pre * (1.0 + tangent)).astype(BF16)
        slope = 0.5 * (1.0 + tangent) + 0.5 * pre * (1.0 - tangent * tangent) * 0.7978845608028654 * (
            1.0 + 3.0 * 0.044715 * pre * pre
        )
        arriving = jnp.concatenate([hidden_grad[at.ws(-j)] for j in groups], axis=0)
        added.fill(groups, hidden, down_buf)
        grad.fill(groups, (arriving * slope).astype(BF16), up_buf)

    spread.forward(2)
    mlp(0)
    mlp(2)
    mlp(1, 3)
    added.far()
    grad.far()
    for j in (1, 3):
        added.near(j)
    for j in (1, 3):
        grad.near(j)
    base_out[...] = summed + added.done()
    normed_grad = grad.done()
    feat_grad[...] = own_rows(row_pair(own_cot, at.tensor)[...], at.tensor) + rstd * (
        normed_grad
        - jnp.mean(normed_grad, axis=-1, keepdims=True)
        - nhat * jnp.mean(normed_grad * nhat, axis=-1, keepdims=True)
    )
    for each in (project, kv, co, up, down, co_x, spread, added, grad):
        each.drain()
    for j in (1, 2, 3):
        ask.copy(j, q_buf.at[at.z], q_buf.at[at.z]).wait_send()
        answer.copy(j, mix16.at[at.zs(j)], mix_back.at[j - 1]).wait_send()
        answer_stat.copy(j, stat.at[at.zs(j)], stat_back.at[j - 1]).wait_send()
        heads.copy(j, mix_send.at[at.xs(j)], mix_recv.at[at.x]).wait_send()
        feats.copy(j, feat16.at[at.ws(j)], feat_recv.at[j - 1]).wait_send()


def body(*args):
    args = list(args)
    args[3] = args[3].reshape(1, 128)
    args[4] = args[4].reshape(1, 128)
    vmem = pl.BlockSpec(memory_space=pltpu.VMEM)
    out = pl.pallas_call(
        kernel,
        out_shape=[jax.ShapeDtypeStruct((8, D), F32)] * 2,
        in_specs=[pl.BlockSpec(memory_space=pltpu.HBM)] * 9,
        out_specs=[vmem] * 2,
        scratch_shapes=[
            pltpu.VMEM((4, 4, 2, 96, 384), BF16),
            pltpu.VMEM((4, 2, 128, 256), BF16),
            pltpu.VMEM((4, 128, 128), BF16),
            pltpu.VMEM((4, 4, 4, 2, 96, 128), BF16),
            pltpu.VMEM((4, 4, 2, 96, 384), BF16),
            pltpu.VMEM((4, 4, 2, 96, 384), BF16),
            pltpu.VMEM((128, D), BF16),
            pltpu.VMEM((2, 1, 128), F32),
            pltpu.VMEM((16, D), BF16),
            pltpu.VMEM((128, D), BF16),
            pltpu.VMEM((128, D), BF16),
            pltpu.VMEM((1024, 512), F32),
            pltpu.VMEM((4, 8, 128), F32),
            pltpu.VMEM((3, 8, 128), F32),
            pltpu.VMEM((4, 128, 128), F32),
            pltpu.VMEM((4, 128, 128), BF16),
            pltpu.VMEM((3, 128, 128), BF16),
            pltpu.VMEM((4, 32, 128), BF16),
            pltpu.VMEM((4, 32, 128), BF16),
            pltpu.VMEM((4, 16, HALF), F32),
            pltpu.VMEM((4, 16, HALF), BF16),
            pltpu.VMEM((3, 16, HALF), BF16),
            pltpu.VMEM((4, 4, 16, HALF), BF16),
            pltpu.VMEM((4, 32, D), BF16),
            pltpu.VMEM((4, 32, 384), F32),
            pltpu.VMEM((2, 4, 4, 16, HALF), BF16),
            pltpu.VMEM((2, 4, 3, 16, HALF), BF16),
            pltpu.VMEM((2, 3, 16, HALF), BF16),
            pltpu.VMEM((2, 3, 16, HALF), BF16),
            pltpu.SemaphoreType.DMA((11,)),
            pltpu.SemaphoreType.DMA((4, 4)),
            pltpu.SemaphoreType.DMA((4, 19)),
            pltpu.SemaphoreType.DMA((7,)),
            pltpu.SemaphoreType.DMA((7,)),
            pltpu.SemaphoreType.DMA((2,)),
            pltpu.SemaphoreType.DMA((15,)),
            pltpu.SemaphoreType.DMA((5, 3)),
            pltpu.SemaphoreType.DMA((5, 3)),
            pltpu.SemaphoreType.DMA((2,)),
            pltpu.SemaphoreType.DMA((2, 12)),
            pltpu.SemaphoreType.DMA((2,)),
            pltpu.SemaphoreType.DMA((2, 4)),
            pltpu.SemaphoreType.DMA((2,)),
            pltpu.SemaphoreType.DMA((16,)),
        ],
        compiler_params=pltpu.CompilerParams(
            collective_id=0, has_side_effects=True, vmem_limit_bytes=64000 * 1024
        ),
    )(*args)
    return tuple(each.astype(BF16) for each in out)


def solution(mesh):
    placed = (
        P("dp", None),
        P(None, "dp", "tensor"),
        P("dp", "tensor"),
        P(),
        P(),
        P("dp", None),
        P("dp", "tensor"),
        P("dp", "tensor"),
        P("dp", None),
    )
    return jax.shard_map(
        body,
        mesh=mesh,
        in_specs=placed,
        out_specs=(P(("dp", "tensor"), None), P(("dp", "tensor"), None)),
        check_vma=False,
    )
```
